32 devices in a mesh: rec: 4 (over y, core), tract: 8 (over z, x).
Axes of the slice: x: 2, y: 2, z: 4, core: 2. Of those that a mesh axis runs over, the one named last changes fastest.
Arguments:
- rep_weights: float32 [80, 131072], P(None, ('rec', 'tract')), may hold values from 0.5 to 2
- covariate_codes: int32 [5, 131072], P(None, ('rec', 'tract')), may hold values from 0 to 15
- tract_of: int32 [131072, 1], P(('rec', 'tract')), may hold values from 0 to 7; in each aligned block of 4096 rows (0 to 4095, 4096 to 8191, ...) at most 1536 rows name the same one
- log_income: bfloat16 [131072], P(('rec', 'tract')), may hold values from -5 to 5
- controls: float32 [64], replicated, may hold values from 7782 to 10240
- threshold_grid: int32 [2048], replicated, may hold values from 0 to 4095
Outputs:
- calibrated: float32 [80, 131072], P(None, ('rec', 'tract'))
- income_tables: float32 [8, 80, 2048], P('tract', None, 'rec')
The draws below stay inside these ranges and needn't reach their ends.
Inputs may be any that keep to these rules, and one draw needn't show every extreme that they name: `tract_of`: among the 4096 persons of one device at most 1536 share a tract; in some aligned blocks of 4096 persons one tract has exactly 1536.
All inputs are finite; a program needn't handle non-finite values.
Results may differ from the reference program's by a relative error of at most 0.0003.
Values may be sent and summed in bfloat16 or wider, within the bound.
A program may use at most 128 MiB of HBM per device.

```python
import math
import jax
import jax.numpy as jnp
import numpy as np
from jax import lax

REPS = 80
CTRL = 64
VARS = 5
THRESH = 2048
R_DEV = 4096
TRACTS = 8
CAP = 1536
TOTAL = 131072


odd_factors = [3, 5, 7, 11]


level_shifts = [1, 6, 11, 3]


copy_limits = [13, 11, 9, 12]


def person_codes(key):
    base_key, pick_key, copy_key = jax.random.split(key, 3)
    first = jax.random.randint(base_key, (TOTAL,), 0, 16, dtype=jnp.int32)
    uniform_codes = jax.random.randint(pick_key, (VARS - 1, TOTAL), 0, 16, dtype=jnp.int32)
    copy_draw = jax.random.randint(copy_key, (VARS - 1, TOTAL), 0, 20, dtype=jnp.int32)
    rows = [first]
    for variable in range(1, VARS):
        table_index = (variable - 1) % 4
        mapped = (first * odd_factors[table_index] + level_shifts[table_index]) % 16
        copied = copy_draw[variable - 1] < copy_limits[table_index]
        rows.append(jnp.where(copied, mapped, uniform_codes[variable - 1]))
    return jnp.stack(rows, axis=0).astype(jnp.int32)


def draw_covariate_codes(key, part):
    return person_codes(jax.random.fold_in(key, 11))


def draw_rep_weights(key, part):
    codes = person_codes(jax.random.fold_in(key, 11))
    own_key = jax.random.fold_in(key, 23)
    level_key, cell_key, noise_key = jax.random.split(own_key, 3)
    levels = jnp.exp(jax.random.uniform(level_key, (REPS, 1), jnp.float32, -0.25, 0.25))
    cells = jnp.exp(jax.random.uniform(cell_key, (REPS, 16), jnp.float32, -0.35, 0.35))
    noise = jnp.exp(jax.random.uniform(noise_key, (REPS, TOTAL), jnp.float32, -0.25, 0.25))
    cell_factor = jnp.take(cells, codes[0], axis=1)
    values = jnp.clip(levels * cell_factor * noise, 0.5, 2.0)
    return values.astype(jnp.float32)


def draw_log_income(key, part):
    first_key = jax.random.fold_in(key, 0)
    values = jnp.clip(jax.random.normal(first_key, (TOTAL,), jnp.float32), -5.0, 5.0)
    return values.astype(jnp.bfloat16)


def plant(values, stream_key, least, top_value):
    longest = values.shape.index(max(values.shape))
    spots = []
    for shift in (0, 1):
        where = [jax.random.randint(jax.random.fold_in(stream_key, axis), (), 0, length) for axis, length in enumerate(values.shape)]
        where[longest] = (where[longest] + shift) % values.shape[longest]
        spots.append(tuple(where))
    return values.at[spots[0]].set(least).at[spots[1]].set(top_value)


def deal_out(key, own, number, rows, amount, top, bound, slope):
    ranking = jax.random.permutation(key, amount)
    packed, usual = load_shares(amount, rows * top, bound, slope, True), load_shares(amount, rows * top, bound, slope, False)
    places = jnp.arange(amount)

    def named(tallies, turn):
        used = int((tallies > 0).sum())
        fixed = max(1, used // 4)
        shifted = fixed + (places - fixed + turn * (used - fixed)) % max(1, amount - fixed)
        return jnp.zeros((amount,), jnp.int32).at[ranking[jnp.where(places < fixed, places, shifted)]].set(jnp.asarray(tallies, jnp.int32))

    tallies = jnp.where(number % 4 == 0, named(packed, number // 4), named(usual, number - number // 4 - 1))
    mixed = jax.random.permutation(jax.random.fold_in(own, 3), amount)
    giver, taker = mixed[0:amount // 2 * 2:2], mixed[1:amount // 2 * 2:2]
    room = jnp.minimum(tallies[giver] - 1, bound - tallies[taker]) // 2
    room = jnp.where((giver == ranking[0]) | (taker == ranking[0]) | (tallies[taker] == 0), 0, jnp.maximum(room, 0))
    shifted = jax.random.randint(jax.random.fold_in(own, 4), (amount // 2,), 0, 1 << 20) % (room + 1)
    tallies = tallies.at[giver].add(-shifted).at[taker].add(shifted)
    labels = jnp.searchsorted(jnp.cumsum(tallies), jnp.arange(rows * top), side="right").astype(jnp.int32)
    listing = labels.reshape(top, rows).T
    listing = listing[jax.random.permutation(jax.random.fold_in(own, 1), rows)]
    turn = jax.random.randint(jax.random.fold_in(own, 2), (rows, 1), 0, top)
    return jnp.take_along_axis(listing, (jnp.arange(top)[None, :] + turn) % top, axis=1)


def load_shares(number_of, total, reach, skew, full):
    portions = [(1 << 20) // math.isqrt(rank ** skew) + 1 for rank in range(1, number_of + 1)]
    largest = reach if full else min(reach, max(-(-total // number_of), total * portions[0] // sum(portions)))
    least = 1 if total - largest >= number_of - 1 else 0
    holding, spare = [largest] + [least] * (number_of - 1), total - largest - least * (number_of - 1)
    while spare > 0:
        free = [i for i in range(1, number_of) if holding[i] < largest] or [i for i in range(1, number_of) if holding[i] < reach]
        pool, left = sum([portions[i] for i in free]), spare
        for i in free:
            more = min(reach - holding[i], max(1, left * portions[i] // pool), spare)
            holding[i] = holding[i] + more
            spare = spare - more
    return np.array(holding)


def setup_inputs(seed: int = 0) -> dict:
    splits = jax.random.split(jax.random.key(seed), 7)
    rep_weights = draw_rep_weights(jax.random.fold_in(splits[6], 71), 0)
    covariate_codes = draw_covariate_codes(jax.random.fold_in(splits[6], 71), 0)
    tract_of_keys = jax.random.split(jax.random.fold_in(splits[2], 1), TOTAL // R_DEV)
    tract_of_turns = jax.random.permutation(jax.random.fold_in(splits[2], 3), TOTAL // R_DEV)
    tract_of = jax.vmap(lambda own, number: deal_out(jax.random.fold_in(splits[2], 2), own, number, R_DEV, TRACTS, 1, CAP, 2))(tract_of_keys, tract_of_turns).reshape((TOTAL, 1))
    log_income = draw_log_income(jax.random.fold_in(splits[6], 71), 0)
    controls = jnp.clip(jax.random.uniform(splits[4], (CTRL,), jnp.float32, 7782.0, 10240.0), 7782.0, 10240.0)
    threshold_grid = plant(jax.random.randint(splits[5], (THRESH,), 0, 4096), jax.random.fold_in(splits[5], 1), 0, 4095).astype(jnp.int32)
    return dict(rep_weights=rep_weights, covariate_codes=covariate_codes, tract_of=tract_of, log_income=log_income, controls=controls, threshold_grid=threshold_grid)


smooth_width = 3.0 / 8192.0
grid_middle = 2048.0
grid_step = 3.0 / 2048.0
base_levels = 16
first_kept = 4

def design(covariate_codes):
    level_codes = jnp.arange(base_levels, dtype=jnp.int32)
    kept_levels = jnp.arange(first_kept, base_levels, dtype=jnp.int32)
    groups = [covariate_codes[0][None, :] == level_codes[:, None]]
    for variable in range(1, covariate_codes.shape[0]):
        groups.append(covariate_codes[variable][None, :] == kept_levels[:, None])
    return jnp.concatenate(groups, axis=0).astype(jnp.float32)

def kept_columns(variables):
    columns_list = list(range(base_levels))
    for variable in range(1, variables):
        columns_list += [variable * base_levels + level_code for level_code in range(first_kept, base_levels)]
    return np.array(columns_list, dtype=np.int32)

def solve_controls(gram_sums, totals, controls):
    factor = jnp.linalg.cholesky(gram_sums)
    gap = (controls[None, :] - totals)[:, :, None]
    middle = lax.linalg.triangular_solve(factor, gap, left_side=True, lower=True)
    result = lax.linalg.triangular_solve(factor, middle, left_side=True, lower=True, transpose_a=True)
    return result[:, :, 0]

def reference(rep_weights, covariate_codes, tract_of, log_income, controls, threshold_grid):
    weights_rows = rep_weights.T
    width = VARS * base_levels
    whole_gram = jnp.zeros((width, width, REPS), jnp.float32)
    single_sums = []
    for first_var in range(VARS):
        single_sums.append(jax.ops.segment_sum(weights_rows, covariate_codes[first_var], num_segments=base_levels))
        for second_var in range(VARS):
            joint = covariate_codes[first_var] * base_levels + covariate_codes[second_var]
            joint_sums = jax.ops.segment_sum(weights_rows, joint, num_segments=base_levels * base_levels)
            whole_gram = whole_gram.at[first_var * base_levels:(first_var + 1) * base_levels, second_var * base_levels:(second_var + 1) * base_levels].set(joint_sums.reshape(base_levels, base_levels, REPS))
    chosen = kept_columns(VARS)
    gram_sums = jnp.transpose(whole_gram[chosen][:, chosen], (2, 0, 1))
    totals = jnp.concatenate(single_sums, axis=0)[chosen].T
    multipliers = solve_controls(gram_sums, totals, controls)
    design_rows = design(covariate_codes)
    factors = 1.0 + jnp.dot(multipliers, design_rows, precision=lax.Precision.HIGHEST)
    calibrated = rep_weights * factors
    sent_weights = calibrated.astype(jnp.bfloat16)
    centers = (threshold_grid.astype(jnp.float32) - grid_middle) * grid_step
    tract_ids = tract_of[:, 0]
    sorted_rows = jnp.argsort(tract_ids, stable=True).astype(jnp.int32)
    sorted_weights = jnp.take(sent_weights, sorted_rows, axis=1)
    sorted_income = jnp.take(log_income, sorted_rows).astype(jnp.float32)
    sorted_tracts = jnp.take(tract_ids, sorted_rows)
    block_rows = math.gcd(TOTAL, 4096)
    block_count = TOTAL // block_rows
    weight_blocks = jnp.transpose(sorted_weights.reshape(REPS, block_count, block_rows), (1, 0, 2))
    income_blocks = sorted_income.reshape(block_count, block_rows)
    tract_blocks = sorted_tracts.reshape(block_count, block_rows)

    def block_step(table_sum, block_data):
        weight_block, income_block, tract_block = block_data
        smoothed = jax.nn.sigmoid((centers[None, :] - income_block[:, None]) / smooth_width).astype(jnp.bfloat16)
        smooth_f32 = smoothed.astype(jnp.float32)
        weights_f32 = weight_block.astype(jnp.float32)
        last_tract = tract_block[block_rows - 1]

        def more_tracts(state):
            return state[0] <= last_tract

        def add_tract(state):
            tract_index, running = state
            in_tract = tract_block == tract_index
            addition = jnp.dot(jnp.where(in_tract[None, :], weights_f32, 0.0).astype(jnp.float32), smooth_f32.astype(jnp.float32), preferred_element_type=jnp.float32)
            return (tract_index + 1, running.at[tract_index].add(addition))
        state = lax.while_loop(more_tracts, add_tract, (tract_block[0], table_sum))
        return (state[1], None)
    start_table = jnp.zeros((TRACTS, REPS, THRESH), jnp.float32)
    table_sum, _ = lax.scan(block_step, start_table, (weight_blocks, income_blocks, tract_blocks))
    income_tables = table_sum / float(TOTAL // TRACTS)
    return (calibrated, income_tables)
```

```python
import functools

import jax
import jax.numpy as jnp
from jax import lax
from jax.experimental import pallas as pl
from jax.experimental.pallas import tpu as pltpu
from jax.sharding import PartitionSpec as P

smooth_width = 3.0 / 8192.0
grid_middle = 2048.0
grid_step = 3.0 / 2048.0
half_scale = 0.5 / smooth_width
base_levels = 16
first_kept = 4
kept = base_levels - first_kept
lanes = 128
bf16 = jnp.bfloat16
f32 = jnp.float32
vmem_bytes = 60 * 1024 * 1024


def firsts_of(variables):
    return [0] + [first_kept] * (variables - 1)


def pair_layout(variables):
    offsets, row = {}, 0
    for u, first in enumerate(firsts_of(variables)):
        for v in range(u + 1, variables):
            offsets[u, v] = row
            row += (base_levels - first) * kept
    return offsets, row, row + base_levels


def split3(value, axis):
    high = value.astype(bf16)
    rest = value - high.astype(f32)
    middle = rest.astype(bf16)
    low = (rest - middle.astype(f32)).astype(bf16)
    return jnp.concatenate([high, middle, low], axis=axis)


def one_hot(key, rows):
    row = lax.broadcasted_iota(jnp.int32, (rows, key.shape[1]), 0)
    return jnp.where(row == key, 1.0, 0.0).astype(bf16)


def remote(source, target, send_sem, recv_sem, where):
    return pltpu.make_async_remote_copy(
        src_ref=source,
        dst_ref=target,
        send_sem=send_sem,
        recv_sem=recv_sem,
        device_id=where,
        device_id_type=pl.DeviceIdType.MESH,
    )


def solve(variables, sums, controls_ref, mat, rhs, coef, sol):
    size = mat.shape[0]
    offsets, singles, _ = pair_layout(variables)
    firsts = firsts_of(variables)
    starts = [0] + [base_levels + kept * (v - 1) for v in range(1, variables)]
    mat[...] = jnp.zeros_like(mat)
    for v in range(variables):
        count = base_levels - firsts[v]
        if v == 0:
            single = sums[singles : singles + count, :]
        else:
            at = offsets[0, v]
            single = sums[at : at + kept, :]
            for c in range(1, base_levels):
                single = single + sums[at + c * kept : at + (c + 1) * kept, :]
        rhs[starts[v] : starts[v] + count, :] = (
            controls_ref[starts[v] : starts[v] + count, :] - single
        )
        for c in range(count):
            mat[starts[v] + c, starts[v] + c : starts[v] + c + 1, :] = single[c : c + 1, :]
    for (u, v), row in offsets.items():
        for c in range(base_levels - firsts[u]):
            at = row + c * kept
            mat[starts[u] + c, starts[v] : starts[v] + kept, :] = sums[at : at + kept, :]

    for block in range(size // 8):
        low = block * 8

        def eliminate(inner, carry, low=low, block=block):
            k = low + inner
            row = mat[k, low:, :]
            pivot = mat[k, pl.ds(k, 1), :]
            place = lax.broadcasted_iota(jnp.int32, row.shape, 0) + low
            factor = jnp.where(place > k, row * (1.0 / pivot), 0.0)
            coef[low:, :] = factor
            rhs[low:, :] = rhs[low:, :] - factor * rhs[pl.ds(k, 1), :]
            for other in range(block, size // 8):
                part = row[other * 8 - low :, :]
                for i in range(other * 8, other * 8 + 8):
                    mat[i, other * 8 :, :] = mat[i, other * 8 :, :] - coef[i : i + 1, :] * part
            return carry

        lax.fori_loop(0, 8, eliminate, 0)

    sol[...] = jnp.zeros_like(sol)
    for block in reversed(range(size // 8)):
        low = block * 8

        def substitute(inner, carry, low=low):
            k = low + 7 - inner
            known = jnp.sum(mat[k, low:, :] * sol[low:, :], axis=0, keepdims=True)
            sol[pl.ds(k, 1), :] = (rhs[pl.ds(k, 1), :] - known) / mat[k, pl.ds(k, 1), :]
            return carry

        lax.fori_loop(0, 8, substitute, 0)

    parts = []
    for v in range(variables):
        count = base_levels - firsts[v]
        if firsts[v]:
            parts.append(jnp.zeros((firsts[v], sol.shape[1]), f32))
        parts.append(sol[starts[v] : starts[v] + count, :])
    return jnp.concatenate(parts, axis=0)


gram_block = 1024
smooth_block = 512
table_block = 1024


def kernel(
    ny, tracts, nx, scale,
    w_ref, codes_ref, tract_ref, income_ref, controls_ref, grid_ref,
    cal_ref, tab_ref,
    pieces, pairs, acc, gram, from_sister, from_chip, final, sums, mat, rhs, coef, sol, x3,
    about, others, corner, cen, smooth, design, sent, masked, table, from_x, over_x, from_z,
    about_sems, other_sems, sister_sems, send_chip, recv_chip, send_back, recv_back,
    final_sems, x_sems, z_sems,
):
    reps, people = w_ref.shape
    variables = codes_ref.shape[0]
    nz = tracts // nx
    blocks = 2 * ny
    chips = ny * tracts
    half = reps // 2
    tiles = gram.shape[1]
    offsets, singles, rows = pair_layout(variables)
    firsts = firsts_of(variables)
    share = smooth.shape[0]
    width = share // 2

    rec, tract = lax.axis_index("rec"), lax.axis_index("tract")
    y, core = lax.div(rec, 2), lax.rem(rec, 2)
    z, x = lax.div(tract, nx), lax.rem(tract, nx)
    sister = {"rec": 2 * y + 1 - core}
    shift = tracts - 2
    chip = y * tracts + lax.rem(tract + shift, tracts)

    def chip_at(number):
        return {
            "rec": 2 * lax.div(number, tracts) + core,
            "tract": lax.rem(lax.rem(number, tracts) + tracts - shift, tracts),
        }

    def each_other(count, body):
        def step(d, carry):
            body(lax.rem(chip + d, count))
            return carry

        lax.fori_loop(1, count, step, 0)

    barrier = pltpu.get_barrier_semaphore()
    pl.semaphore_signal(barrier, inc=1, device_id=sister, device_id_type=pl.DeviceIdType.MESH)
    each_other(
        chips,
        lambda peer: pl.semaphore_signal(
            barrier, inc=1, device_id=chip_at(peer), device_id_type=pl.DeviceIdType.MESH
        ),
    )

    about[0, 0:variables, :] = codes_ref[...].astype(f32)
    about[0, variables : variables + 1, :] = tract_ref[...].astype(f32)
    about[0, variables + 1 : variables + 2, :] = income_ref[...].astype(f32)
    about[0, variables + 2 :, :] = jnp.zeros((about.shape[1] - variables - 2, people), f32)
    pieces[...] = split3(w_ref[...], 0)

    pl.semaphore_wait(barrier, chips)

    def spread(source, slot, sems):
        return [remote(source, slot(1), sems.at[0, 1], sems.at[1, 1], sister)] + [
            remote(
                source,
                slot(2 * e),
                sems.at[0, 2 * e],
                sems.at[1, 2 * e],
                {"rec": 2 * lax.rem(y - e + ny, ny) + core},
            )
            for e in range(1, ny)
        ]

    def relay(slot, sems):
        return [
            remote(
                slot(2 * e), slot(2 * e + 1), sems.at[0, 2 * e + 1], sems.at[1, 2 * e + 1], sister
            )
            for e in range(1, ny)
        ]

    about_slot = lambda b: about.at[b]
    other_slot = lambda b: others.at[b - 1]
    about_copies = spread(about.at[0], about_slot, about_sems)
    other_copies = spread(w_ref, other_slot, other_sems)
    for copy in about_copies:
        copy.start()
    for copy in other_copies:
        copy.start()

    cut = offsets[1, 2] // lanes
    chunks = [(0, cut), (cut, tiles)]

    def gram_chunk(first, last):
        low, high = first * lanes, last * lanes
        groups = []
        for (u, v), row in offsets.items():
            if low <= row < high:
                groups.append((u, v, row - low, (base_levels - firsts[u]) * kept))
        acc[:, : high - low] = jnp.zeros((acc.shape[0], high - low), f32)

        def body(i, carry):
            cols = pl.ds(pl.multiple_of(i * gram_block, gram_block), gram_block)
            for u, v, row, count in groups:
                right = codes_ref[v : v + 1, cols] - first_kept
                key = (codes_ref[u : u + 1, cols] - firsts[u]) * kept + right
                key = jnp.where(right < 0, -1, key)
                pairs[row : row + count, :] = one_hot(key, count)
            if low <= singles < high:
                pairs[singles - low : high - low, :] = one_hot(
                    codes_ref[0:1, cols], high - singles
                )
            acc[:, : high - low] += lax.dot_general(
                pieces[:, cols],
                pairs[: high - low, :],
                (((1,), (1,)), ((), ())),
                preferred_element_type=f32,
            )
            return carry

        lax.fori_loop(0, people // gram_block, body, 0)
        for t in range(first, last):
            at = slice((t - first) * lanes, (t - first + 1) * lanes)
            value = acc[:reps, at] + acc[reps : 2 * reps, at] + acc[2 * reps :, at]
            gram[0, t] = value[:half]
            gram[1, t] = value[half:]

    def to_sister(c):
        first, last = chunks[c]
        return remote(
            gram.at[1 - core, first:last],
            from_sister.at[first:last],
            sister_sems.at[0, c],
            sister_sems.at[1, c],
            sister,
        )

    def to_chips(c):
        first, last = chunks[c]
        to_sister(c).wait_recv()
        for t in range(first, last):
            gram[core, t] = gram[core, t] + from_sister[t]

        def start(peer):
            @pl.when((peer >= first) & (peer < last))
            def _():
                remote(
                    gram.at[core, peer],
                    from_chip.at[chip],
                    send_chip.at[peer],
                    recv_chip.at[chip],
                    chip_at(peer),
                ).start()

        each_other(chips, start)

    def smooth_part(b, first, last):
        def body(i, carry):
            start = pl.multiple_of(i * smooth_block, smooth_block)
            cols = pl.ds(start, smooth_block)
            there = pl.ds(pl.multiple_of(b * people + start, smooth_block), smooth_block)
            income = about[b, variables + 1 : variables + 2, cols] * half_scale
            centers = jnp.concatenate([cen[...]] * (smooth_block // lanes), axis=1)
            smooth[:, there] = (0.5 + 0.5 * jnp.tanh(centers - income)).astype(bf16)
            for v in range(variables):
                code = about[b, v : v + 1, cols].astype(jnp.int32)
                design[v * base_levels : (v + 1) * base_levels, there] = one_hot(code, base_levels)
            return carry

        lax.fori_loop(first, last, body, 0)

    steps = people // smooth_block

    gram_chunk(*chunks[0])
    to_sister(0).start()
    gram_chunk(*chunks[1])
    to_sister(1).start()
    to_chips(0)

    corner[...] = jnp.zeros_like(corner)
    count = share // lanes
    corner[:count, :] = (
        (grid_ref[pl.ds(rec * count, count), :].astype(f32) - grid_middle)
        * (grid_step * half_scale)
    )
    turned = corner[...].T
    for i in range(count):
        cen[i * lanes : (i + 1) * lanes, :] = jnp.broadcast_to(turned[:, i : i + 1], (lanes, lanes))

    about_relay = relay(about_slot, about_sems)
    to_chips(1)
    smooth_part(0, 0, steps)
    for e in range(1, ny):
        about_copies[e].wait_recv()
        about_relay[e - 1].start()

    @pl.when(chip < tiles)
    def _():
        each_other(
            chips,
            lambda peer: remote(
                gram.at[core, 0], from_chip.at[peer], send_chip.at[0], recv_chip.at[peer], sister
            ).wait_recv(),
        )
        total = lax.fori_loop(
            1,
            chips,
            lambda d, value: value + from_chip[lax.rem(chip + d, chips)],
            gram[core, chip],
        )
        final[core, chip] = total
        each_other(
            chips,
            lambda peer: remote(
                final.at[core, chip],
                final.at[core, chip],
                send_back.at[peer],
                recv_back.at[chip],
                chip_at(peer),
            ).start(),
        )

    about_copies[0].wait_recv()
    smooth_part(1, 0, steps)

    def hand_over(t):
        return remote(
            final.at[core, t], final.at[core, t], final_sems.at[0, t], final_sems.at[1, t], sister
        )

    def taken(t):
        return remote(
            final.at[core, t],
            final.at[1 - core, t],
            final_sems.at[0, t],
            final_sems.at[1, t],
            sister,
        )

    for t in range(tiles):
        @pl.when(chip != t)
        def _():
            remote(
                final.at[core, t], final.at[core, t], send_back.at[0], recv_back.at[t], sister
            ).wait_recv()

        hand_over(t).start()
    for e in range(1, ny):
        smooth_part(2 * e, 0, steps)
        about_relay[e - 1].wait_recv()
        smooth_part(2 * e + 1, 0, steps)
    for t in range(tiles):
        taken(t).wait_recv()
        whole = jnp.concatenate([final[0, t], final[1, t]], axis=0)
        sums[t * lanes : (t + 1) * lanes, :] = whole.T

    x3[...] = split3(solve(variables, sums, controls_ref, mat, rhs, coef, sol), 0)

    other_relay = relay(other_slot, other_sems)
    for e in range(1, ny):
        other_copies[e].wait_recv()
        other_relay[e - 1].start()

    def table_pass(part):
        table[part] = jnp.zeros(table.shape[1:], f32)
        for b in range(blocks):
            if part == 0 and b > 0:
                if b % 2 == 1:
                    (other_copies[0] if b == 1 else other_relay[b // 2 - 1]).wait_recv()

            def body(i, carry, b=b):
                start = pl.multiple_of(i * table_block, table_block)
                cols = pl.ds(start, table_block)
                there = pl.ds(pl.multiple_of(b * people + start, table_block), table_block)
                if part == 0:
                    adjustment = lax.dot_general(
                        x3[...],
                        jnp.concatenate([design[:, there]] * 3, axis=0),
                        (((0,), (0,)), ((), ())),
                        preferred_element_type=f32,
                    )
                    weights = w_ref[:, cols] if b == 0 else others[b - 1, :, cols]
                    calibrated = weights * (1.0 + adjustment)
                    if b == 0:
                        cal_ref[:, cols] = calibrated
                    sent[:, there] = calibrated.astype(bf16)
                own = about[b, variables : variables + 1, cols]
                value = sent[:, there]
                for k in range(tracts):
                    at = (k % nx * nz + k // nx) * reps
                    inside = jnp.where(own == float(k), 1.0, 0.0).astype(bf16)
                    masked[at : at + reps, :] = value * inside
                table[part] += lax.dot_general(
                    masked[...],
                    smooth[part * width : (part + 1) * width, there],
                    (((1,), (1,)), ((), ())),
                    preferred_element_type=f32,
                )
                return carry

            lax.fori_loop(0, people // table_block, body, 0)

    deep = nz * reps

    def across_x(part, e):
        to = lax.rem(x + e, nx)
        return remote(
            table.at[part, pl.ds(pl.multiple_of(to * deep, 8), deep)],
            from_x.at[part, e - 1],
            x_sems.at[0, part, e],
            x_sems.at[1, part, e],
            {"tract": z * nx + to},
        )

    def along_z(part, e):
        to = lax.rem(z + e, nz)
        return remote(
            over_x.at[part, pl.ds(pl.multiple_of(to * reps, 8), reps)],
            from_z.at[part, e - 1],
            z_sems.at[0, part, e],
            z_sems.at[1, part, e],
            {"tract": to * nx + x},
        )

    for part in range(2):
        table_pass(part)
        for e in range(1, nx):
            across_x(part, e).start()
    for part in range(2):
        value = table[part, pl.ds(pl.multiple_of(x * deep, 8), deep), :]
        for e in range(1, nx):
            across_x(part, e).wait_recv()
            value = value + from_x[part, e - 1]
        over_x[part] = value
        for e in range(1, nz):
            along_z(part, e).start()
    for part in range(2):
        value = over_x[part, pl.ds(pl.multiple_of(z * reps, 8), reps), :]
        for e in range(1, nz):
            along_z(part, e).wait_recv()
            value = value + from_z[part, e - 1]
        tab_ref[0, :, part * width : (part + 1) * width] = value / scale

    for copy in about_copies + about_relay + other_copies + other_relay:
        copy.wait_send()
    for c in range(2):
        to_sister(c).wait_send()

    def left(peer):
        @pl.when(peer < tiles)
        def _():
            remote(
                gram.at[core, peer], from_chip.at[chip], send_chip.at[peer], recv_chip.at[chip],
                chip_at(peer),
            ).wait_send()

        @pl.when(chip < tiles)
        def _():
            remote(
                final.at[core, chip], final.at[core, chip], send_back.at[peer], recv_back.at[chip],
                chip_at(peer),
            ).wait_send()

    each_other(chips, left)
    for t in range(tiles):
        hand_over(t).wait_send()
    for part in range(2):
        for e in range(1, nx):
            across_x(part, e).wait_send()
        for e in range(1, nz):
            along_z(part, e).wait_send()


def shards(rep_weights, covariate_codes, tract_of, log_income, controls, threshold_grid):
    reps, people = rep_weights.shape
    variables = covariate_codes.shape[0]
    tracts = lax.axis_size("tract")
    recs = lax.axis_size("rec")
    ny = recs // 2
    nz = 4
    nx = tracts // nz
    chips = ny * tracts
    share = threshold_grid.shape[0] // recs
    width = share // 2
    size = controls.shape[0]
    rows = pair_layout(variables)[2]
    tiles = -(-rows // lanes)
    cut = pair_layout(variables)[0][1, 2] // lanes
    most = max(cut, tiles - cut) * lanes
    designs = variables * base_levels
    vmem = pltpu.VMEM
    dma = pltpu.SemaphoreType.DMA
    return pl.pallas_call(
        functools.partial(kernel, ny, tracts, nx, float(people * recs)),
        in_specs=[pl.BlockSpec(memory_space=vmem)] * 6,
        out_specs=[pl.BlockSpec(memory_space=vmem)] * 2,
        out_shape=[
            jax.ShapeDtypeStruct((reps, people), f32),
            jax.ShapeDtypeStruct((1, reps, share), f32),
        ],
        scratch_shapes=[
            vmem((3 * reps, people), bf16),
            vmem((most, gram_block), bf16),
            vmem((3 * reps, most), f32),
            vmem((2, tiles, reps // 2, lanes), f32),
            vmem((tiles, reps // 2, lanes), f32),
            vmem((chips, reps // 2, lanes), f32),
            vmem((2, tiles, reps // 2, lanes), f32),
            vmem((tiles * lanes, reps), f32),
            vmem((size, size, reps), f32),
            vmem((size, reps), f32),
            vmem((size, reps), f32),
            vmem((size, reps), f32),
            vmem((3 * designs, reps), bf16),
            vmem((recs, 8, people), f32),
            vmem((recs - 1, reps, people), f32),
            vmem((8, lanes), f32),
            vmem((share, lanes), f32),
            vmem((share, recs * people), bf16),
            vmem((designs, recs * people), bf16),
            vmem((reps, recs * people), bf16),
            vmem((tracts * reps, table_block), bf16),
            vmem((2, tracts * reps, width), f32),
            vmem((2, nx - 1, nz * reps, width), f32),
            vmem((2, nz * reps, width), f32),
            vmem((2, nz - 1, reps, width), f32),
            dma((2, recs)),
            dma((2, recs)),
            dma((2, 2)),
            dma((tiles,)),
            dma((chips,)),
            dma((chips,)),
            dma((tiles,)),
            dma((2, tiles)),
            dma((2, 2, nx)),
            dma((2, 2, nz)),
        ],
        compiler_params=pltpu.CompilerParams(
            vmem_limit_bytes=vmem_bytes, collective_id=0, has_side_effects=True
        ),
    )(
        rep_weights,
        covariate_codes,
        tract_of.reshape(1, people),
        log_income.astype(f32).reshape(1, people),
        jnp.broadcast_to(controls[:, None], (size, reps)),
        threshold_grid.reshape(-1, lanes),
    )


def solution(mesh):
    placed = (
        P(None, ("rec", "tract")),
        P(None, ("rec", "tract")),
        P(("rec", "tract"), None),
        P(("rec", "tract")),
        P(),
        P(),
    )
    return jax.shard_map(
        shards,
        mesh=mesh,
        in_specs=placed,
        out_specs=(P(None, ("rec", "tract")), P("tract", None, "rec")),
        check_vma=False,
    )
```

```python
import functools

import jax
import jax.numpy as jnp
from jax import lax
from jax.experimental import pallas as pl
from jax.experimental.pallas import tpu as pltpu
from jax.sharding import PartitionSpec as P

smooth_width = 3.0 / 8192.0
grid_middle = 2048.0
grid_step = 3.0 / 2048.0
half_scale = 0.5 / smooth_width
base_levels = 16
first_kept = 4
kept = base_levels - first_kept
lanes = 128
bf16 = jnp.bfloat16
f32 = jnp.float32
vmem_bytes = 60 * 1024 * 1024


def firsts_of(variables):
    return [0] + [first_kept] * (variables - 1)


def pair_layout(variables):
    offsets, row = {}, 0
    for u, first in enumerate(firsts_of(variables)):
        for v in range(u + 1, variables):
            offsets[u, v] = row
            row += (base_levels - first) * kept
    return offsets, row, row + base_levels


def split3(value, axis):
    high = value.astype(bf16)
    rest = value - high.astype(f32)
    middle = rest.astype(bf16)
    low = (rest - middle.astype(f32)).astype(bf16)
    return jnp.concatenate([high, middle, low], axis=axis)


def one_hot(key, rows):
    row = lax.broadcasted_iota(jnp.int32, (rows, key.shape[1]), 0)
    return jnp.where(row == key, 1.0, 0.0).astype(bf16)


def remote(source, target, send_sem, recv_sem, where):
    return pltpu.make_async_remote_copy(
        src_ref=source,
        dst_ref=target,
        send_sem=send_sem,
        recv_sem=recv_sem,
        device_id=where,
        device_id_type=pl.DeviceIdType.MESH,
    )


def solve(variables, sums, controls_ref, mat, rhs, coef, sol):
    size = mat.shape[0]
    offsets, singles, _ = pair_layout(variables)
    firsts = firsts_of(variables)
    starts = [0] + [base_levels + kept * (v - 1) for v in range(1, variables)]
    mat[...] = jnp.zeros_like(mat)
    for v in range(variables):
        count = base_levels - firsts[v]
        if v == 0:
            single = sums[singles : singles + count, :]
        else:
            at = offsets[0, v]
            single = sums[at : at + kept, :]
            for c in range(1, base_levels):
                single = single + sums[at + c * kept : at + (c + 1) * kept, :]
        rhs[starts[v] : starts[v] + count, :] = (
            controls_ref[starts[v] : starts[v] + count, :] - single
        )
        for c in range(count):
            mat[starts[v] + c, starts[v] + c : starts[v] + c + 1, :] = single[c : c + 1, :]
    for (u, v), row in offsets.items():
        for c in range(base_levels - firsts[u]):
            at = row + c * kept
            mat[starts[u] + c, starts[v] : starts[v] + kept, :] = sums[at : at + kept, :]

    for block in range(size // 8):
        low = block * 8

        def eliminate(inner, carry, low=low, block=block):
            k = low + inner
            row = mat[k, low:, :]
            pivot = mat[k, pl.ds(k, 1), :]
            place = lax.broadcasted_iota(jnp.int32, row.shape, 0) + low
            factor = jnp.where(place > k, row * (1.0 / pivot), 0.0)
            coef[low:, :] = factor
            rhs[low:, :] = rhs[low:, :] - factor * rhs[pl.ds(k, 1), :]
            for other in range(block, size // 8):
                part = row[other * 8 - low :, :]
                for i in range(other * 8, other * 8 + 8):
                    mat[i, other * 8 :, :] = mat[i, other * 8 :, :] - coef[i : i + 1, :] * part
            return carry

        lax.fori_loop(0, 8, eliminate, 0)

    sol[...] = jnp.zeros_like(sol)
    for block in reversed(range(size // 8)):
        low = block * 8

        def substitute(inner, carry, low=low):
            k = low + 7 - inner
            known = jnp.sum(mat[k, low:, :] * sol[low:, :], axis=0, keepdims=True)
            sol[pl.ds(k, 1), :] = (rhs[pl.ds(k, 1), :] - known) / mat[k, pl.ds(k, 1), :]
            return carry

        lax.fori_loop(0, 8, substitute, 0)

    parts = []
    for v in range(variables):
        count = base_levels - firsts[v]
        if firsts[v]:
            parts.append(jnp.zeros((firsts[v], sol.shape[1]), f32))
        parts.append(sol[starts[v] : starts[v] + count, :])
    return jnp.concatenate(parts, axis=0)


gram_block = 1024
smooth_block = 512
quarter = 1024
low_weight, high_weight = 0.5, 2.0
code_step = (high_weight - low_weight) / 65535.0
table_block = quarter


def kernel(
    ny, tracts, nx, scale,
    w_ref, codes_ref, tract_ref, income_ref, controls_ref, grid_ref,
    cal_ref, tab_ref,
    pieces, pairs, acc, gram, from_sister, from_chip, final, sums, mat, rhs, coef, sol, x3,
    about, coded, others, located, corner, cen, smooth, design, sent, masked, table, from_x, over_x, from_z,
    about_sems, other_sems, sister_sems, send_chip, recv_chip, send_back, recv_back,
    final_sems, x_sems, z_sems,
):
    reps, people = w_ref.shape
    variables = codes_ref.shape[0]
    nz = tracts // nx
    blocks = 2 * ny
    chips = ny * tracts
    half = reps // 2
    tiles = gram.shape[1]
    offsets, singles, rows = pair_layout(variables)
    firsts = firsts_of(variables)
    share = smooth.shape[0]
    width = share // 2

    rec, tract = lax.axis_index("rec"), lax.axis_index("tract")
    y, core = lax.div(rec, 2), lax.rem(rec, 2)
    z, x = lax.div(tract, nx), lax.rem(tract, nx)
    sister = {"rec": 2 * y + 1 - core}
    shift = tracts - 2
    chip = y * tracts + lax.rem(tract + shift, tracts)

    def chip_at(number):
        return {
            "rec": 2 * lax.div(number, tracts) + core,
            "tract": lax.rem(lax.rem(number, tracts) + tracts - shift, tracts),
        }

    def each_other(count, body):
        def step(d, carry):
            body(lax.rem(chip + d, count))
            return carry

        lax.fori_loop(1, count, step, 0)

    barrier = pltpu.get_barrier_semaphore()
    pl.semaphore_signal(barrier, inc=1, device_id=sister, device_id_type=pl.DeviceIdType.MESH)
    each_other(
        chips,
        lambda peer: pl.semaphore_signal(
            barrier, inc=1, device_id=chip_at(peer), device_id_type=pl.DeviceIdType.MESH
        ),
    )

    located[0, 0:variables, :] = codes_ref[...].astype(f32)
    located[0, variables : variables + 1, :] = tract_ref[...].astype(f32)
    located[0, variables + 1 : variables + 2, :] = income_ref[...]
    located[0, variables + 2 :, :] = jnp.zeros((located.shape[1] - variables - 2, people), f32)
    about[0] = jnp.concatenate(
        [located[0, :, : people // 2], located[0, :, people // 2 :]], axis=0
    ).astype(bf16)
    for q in range(people // quarter):
        part = w_ref[:, q * quarter : (q + 1) * quarter]
        coded[q] = jnp.round((part - low_weight) / code_step - 32768.0).astype(jnp.int32).astype(jnp.int16)
    pieces[...] = split3(w_ref[...], 0)

    pl.semaphore_wait(barrier, chips)

    def spread(source, slot, sems):
        return [remote(source, slot(1), sems.at[0, 1], sems.at[1, 1], sister)] + [
            remote(
                source,
                slot(2 * e),
                sems.at[0, 2 * e],
                sems.at[1, 2 * e],
                {"rec": 2 * lax.rem(y - e + ny, ny) + core},
            )
            for e in range(1, ny)
        ]

    def relay(slot, sems):
        return [
            remote(
                slot(2 * e), slot(2 * e + 1), sems.at[0, 2 * e + 1], sems.at[1, 2 * e + 1], sister
            )
            for e in range(1, ny)
        ]

    about_slot = lambda b: about.at[b]
    quarters = people // quarter

    def other_slot(q):
        return lambda b: others.at[b - 1, q]

    about_copies = spread(about.at[0], about_slot, about_sems)
    other_copies = [
        spread(coded.at[q], other_slot(q), other_sems.at[q]) for q in range(quarters)
    ]
    about_relay = relay(about_slot, about_sems)
    other_relay = [relay(other_slot(q), other_sems.at[q]) for q in range(quarters)]
    for copy in about_copies[1:] + about_copies[:1]:
        copy.start()

    def start_over_y(first, last):
        for q in range(first, last):
            for copy in other_copies[q][1:]:
                copy.start()

    start_over_y(0, quarters // 2)
    for q in range(quarters):
        other_copies[q][0].start()

    cut = offsets[1, 2] // lanes
    chunks = [(0, cut), (cut, tiles)]

    def gram_chunk(first, last):
        low, high = first * lanes, last * lanes
        groups = []
        for (u, v), row in offsets.items():
            if low <= row < high:
                groups.append((u, v, row - low, (base_levels - firsts[u]) * kept))
        acc[:, : high - low] = jnp.zeros((acc.shape[0], high - low), f32)

        def body(i, carry):
            cols = pl.ds(pl.multiple_of(i * gram_block, gram_block), gram_block)
            for u, v, row, count in groups:
                right = codes_ref[v : v + 1, cols] - first_kept
                key = (codes_ref[u : u + 1, cols] - firsts[u]) * kept + right
                key = jnp.where(right < 0, -1, key)
                pairs[row : row + count, :] = one_hot(key, count)
            if low <= singles < high:
                pairs[singles - low : high - low, :] = one_hot(
                    codes_ref[0:1, cols], high - singles
                )
            acc[:, : high - low] += lax.dot_general(
                pieces[:, cols],
                pairs[: high - low, :],
                (((1,), (1,)), ((), ())),
                preferred_element_type=f32,
            )
            return carry

        lax.fori_loop(0, people // gram_block, body, 0)
        for t in range(first, last):
            at = slice((t - first) * lanes, (t - first + 1) * lanes)
            value = acc[:reps, at] + acc[reps : 2 * reps, at] + acc[2 * reps :, at]
            gram[0, t] = value[:half]
            gram[1, t] = value[half:]

    def to_sister(c):
        first, last = chunks[c]
        return remote(
            gram.at[1 - core, first:last],
            from_sister.at[first:last],
            sister_sems.at[0, c],
            sister_sems.at[1, c],
            sister,
        )

    def to_chips(c):
        first, last = chunks[c]
        to_sister(c).wait_recv()
        for t in range(first, last):
            gram[core, t] = gram[core, t] + from_sister[t]

        def start(peer):
            @pl.when((peer >= first) & (peer < last))
            def _():
                remote(
                    gram.at[core, peer],
                    from_chip.at[chip],
                    send_chip.at[peer],
                    recv_chip.at[chip],
                    chip_at(peer),
                ).start()

        each_other(chips, start)

    def smooth_part(b, first, last):
        if b > 0:
            value = about[b].astype(f32)
            located[b, :, : people // 2] = value[: value.shape[0] // 2]
            located[b, :, people // 2 :] = value[value.shape[0] // 2 :]

        def body(i, carry):
            start = pl.multiple_of(i * smooth_block, smooth_block)
            cols = pl.ds(start, smooth_block)
            there = pl.ds(pl.multiple_of(b * people + start, smooth_block), smooth_block)
            income = located[b, variables + 1 : variables + 2, cols] * half_scale
            centers = jnp.concatenate([cen[...]] * (smooth_block // lanes), axis=1)
            smooth[:, there] = (0.5 + 0.5 * jnp.tanh(centers - income)).astype(bf16)
            for v in range(variables):
                code = located[b, v : v + 1, cols].astype(jnp.int32)
                design[v * base_levels : (v + 1) * base_levels, there] = one_hot(code, base_levels)
            return carry

        lax.fori_loop(first, last, body, 0)

    steps = people // smooth_block

    gram_chunk(*chunks[0])
    to_sister(0).start()
    gram_chunk(*chunks[1])
    to_sister(1).start()
    to_chips(0)

    corner[...] = jnp.zeros_like(corner)
    count = share // lanes
    corner[:count, :] = (
        (grid_ref[pl.ds(rec * count, count), :].astype(f32) - grid_middle)
        * (grid_step * half_scale)
    )
    turned = corner[...].T
    for i in range(count):
        cen[i * lanes : (i + 1) * lanes, :] = jnp.broadcast_to(turned[:, i : i + 1], (lanes, lanes))

    to_chips(1)
    start_over_y(quarters // 2, quarters - 1)
    smooth_part(0, 0, steps)
    for e in range(1, ny):
        about_copies[e].wait_recv()
        about_relay[e - 1].start()

    @pl.when(chip < tiles)
    def _():
        each_other(
            chips,
            lambda peer: remote(
                gram.at[core, 0], from_chip.at[peer], send_chip.at[0], recv_chip.at[peer], sister
            ).wait_recv(),
        )
        total = lax.fori_loop(
            1,
            chips,
            lambda d, value: value + from_chip[lax.rem(chip + d, chips)],
            gram[core, chip],
        )
        final[core, chip] = total
        each_other(
            chips,
            lambda peer: remote(
                final.at[core, chip],
                final.at[core, chip],
                send_back.at[peer],
                recv_back.at[chip],
                chip_at(peer),
            ).start(),
        )

    about_copies[0].wait_recv()
    smooth_part(1, 0, steps)

    def hand_over(t):
        return remote(
            final.at[core, t], final.at[core, t], final_sems.at[0, t], final_sems.at[1, t], sister
        )

    def taken(t):
        return remote(
            final.at[core, t],
            final.at[1 - core, t],
            final_sems.at[0, t],
            final_sems.at[1, t],
            sister,
        )

    for t in range(tiles):
        @pl.when(chip != t)
        def _():
            remote(
                final.at[core, t], final.at[core, t], send_back.at[0], recv_back.at[t], sister
            ).wait_recv()

        hand_over(t).start()
    start_over_y(quarters - 1, quarters)
    for e in range(1, ny):
        smooth_part(2 * e, 0, steps)
        about_relay[e - 1].wait_recv()
        smooth_part(2 * e + 1, 0, steps)
    for t in range(tiles):
        taken(t).wait_recv()
        whole = jnp.concatenate([final[0, t], final[1, t]], axis=0)
        sums[t * lanes : (t + 1) * lanes, :] = whole.T

    x3[...] = split3(solve(variables, sums, controls_ref, mat, rhs, coef, sol), 0)

    for q in range(quarters):
        for e in range(1, ny):
            other_copies[q][e].wait_recv()
            other_relay[q][e - 1].start()

    def table_pass(part):
        table[part] = jnp.zeros(table.shape[1:], f32)
        for b in range(blocks):
            if part == 0 and b > 0:
                if b % 2 == 1:
                    for q in range(quarters):
                        (other_copies[q][0] if b == 1 else other_relay[q][b // 2 - 1]).wait_recv()

            def body(i, carry, b=b):
                start = pl.multiple_of(i * table_block, table_block)
                cols = pl.ds(start, table_block)
                there = pl.ds(pl.multiple_of(b * people + start, table_block), table_block)
                if part == 0:
                    adjustment = lax.dot_general(
                        x3[...],
                        jnp.concatenate([design[:, there]] * 3, axis=0),
                        (((0,), (0,)), ((), ())),
                        preferred_element_type=f32,
                    )
                    if b == 0:
                        weights = w_ref[:, cols]
                    else:
                        code = others[b - 1, i].astype(jnp.int32).astype(f32)
                        weights = (code + 32768.0) * code_step + low_weight
                    calibrated = weights * (1.0 + adjustment)
                    if b == 0:
                        cal_ref[:, cols] = calibrated
                    sent[:, there] = calibrated.astype(bf16)
                own = located[b, variables : variables + 1, cols]
                value = sent[:, there]
                for k in range(tracts):
                    at = (k % nx * nz + k // nx) * reps
                    inside = jnp.where(own == float(k), 1.0, 0.0).astype(bf16)
                    masked[at : at + reps, :] = value * inside
                table[part] += lax.dot_general(
                    masked[...],
                    smooth[part * width : (part + 1) * width, there],
                    (((1,), (1,)), ((), ())),
                    preferred_element_type=f32,
                )
                return carry

            lax.fori_loop(0, people // table_block, body, 0)

    deep = nz * reps

    def across_x(part, e):
        to = lax.rem(x + e, nx)
        return remote(
            table.at[part, pl.ds(pl.multiple_of(to * deep, 8), deep)],
            from_x.at[part, e - 1],
            x_sems.at[0, part, e],
            x_sems.at[1, part, e],
            {"tract": z * nx + to},
        )

    def along_z(part, e):
        to = lax.rem(z + e, nz)
        return remote(
            over_x.at[part, pl.ds(pl.multiple_of(to * reps, 8), reps)],
            from_z.at[part, e - 1],
            z_sems.at[0, part, e],
            z_sems.at[1, part, e],
            {"tract": to * nx + x},
        )

    for part in range(2):
        table_pass(part)
        for e in range(1, nx):
            across_x(part, e).start()
    for part in range(2):
        value = table[part, pl.ds(pl.multiple_of(x * deep, 8), deep), :]
        for e in range(1, nx):
            across_x(part, e).wait_recv()
            value = value + from_x[part, e - 1]
        over_x[part] = value
        for e in range(1, nz):
            along_z(part, e).start()
    for part in range(2):
        value = over_x[part, pl.ds(pl.multiple_of(z * reps, 8), reps), :]
        for e in range(1, nz):
            along_z(part, e).wait_recv()
            value = value + from_z[part, e - 1]
        tab_ref[0, :, part * width : (part + 1) * width] = value / scale

    for copy in about_copies + about_relay + sum(other_copies + other_relay, []):
        copy.wait_send()
    for c in range(2):
        to_sister(c).wait_send()

    def left(peer):
        @pl.when(peer < tiles)
        def _():
            remote(
                gram.at[core, peer], from_chip.at[chip], send_chip.at[peer], recv_chip.at[chip],
                chip_at(peer),
            ).wait_send()

        @pl.when(chip < tiles)
        def _():
            remote(
                final.at[core, chip], final.at[core, chip], send_back.at[peer], recv_back.at[chip],
                chip_at(peer),
            ).wait_send()

    each_other(chips, left)
    for t in range(tiles):
        hand_over(t).wait_send()
    for part in range(2):
        for e in range(1, nx):
            across_x(part, e).wait_send()
        for e in range(1, nz):
            along_z(part, e).wait_send()


def shards(rep_weights, covariate_codes, tract_of, log_income, controls, threshold_grid):
    reps, people = rep_weights.shape
    variables = covariate_codes.shape[0]
    tracts = lax.axis_size("tract")
    recs = lax.axis_size("rec")
    ny = recs // 2
    nz = 4
    nx = tracts // nz
    chips = ny * tracts
    share = threshold_grid.shape[0] // recs
    width = share // 2
    size = controls.shape[0]
    rows = pair_layout(variables)[2]
    tiles = -(-rows // lanes)
    cut = pair_layout(variables)[0][1, 2] // lanes
    most = max(cut, tiles - cut) * lanes
    designs = variables * base_levels
    vmem = pltpu.VMEM
    dma = pltpu.SemaphoreType.DMA
    return pl.pallas_call(
        functools.partial(kernel, ny, tracts, nx, float(people * recs)),
        in_specs=[pl.BlockSpec(memory_space=vmem)] * 6,
        out_specs=[pl.BlockSpec(memory_space=vmem)] * 2,
        out_shape=[
            jax.ShapeDtypeStruct((reps, people), f32),
            jax.ShapeDtypeStruct((1, reps, share), f32),
        ],
        scratch_shapes=[
            vmem((3 * reps, people), bf16),
            vmem((most, gram_block), bf16),
            vmem((3 * reps, most), f32),
            vmem((2, tiles, reps // 2, lanes), f32),
            vmem((tiles, reps // 2, lanes), f32),
            vmem((chips, reps // 2, lanes), f32),
            vmem((2, tiles, reps // 2, lanes), f32),
            vmem((tiles * lanes, reps), f32),
            vmem((size, size, reps), f32),
            vmem((size, reps), f32),
            vmem((size, reps), f32),
            vmem((size, reps), f32),
            vmem((3 * designs, reps), bf16),
            vmem((recs, 16, people // 2), bf16),
            vmem((people // quarter, reps, quarter), jnp.int16),
            vmem((recs - 1, people // quarter, reps, quarter), jnp.int16),
            vmem((recs, 8, people), f32),
            vmem((8, lanes), f32),
            vmem((share, lanes), f32),
            vmem((share, recs * people), bf16),
            vmem((designs, recs * people), bf16),
            vmem((reps, recs * people), bf16),
            vmem((tracts * reps, table_block), bf16),
            vmem((2, tracts * reps, width), f32),
            vmem((2, nx - 1, nz * reps, width), f32),
            vmem((2, nz * reps, width), f32),
            vmem((2, nz - 1, reps, width), f32),
            dma((2, recs)),
            dma((people // quarter, 2, recs)),
            dma((2, 2)),
            dma((tiles,)),
            dma((chips,)),
            dma((chips,)),
            dma((tiles,)),
            dma((2, tiles)),
            dma((2, 2, nx)),
            dma((2, 2, nz)),
        ],
        compiler_params=pltpu.CompilerParams(
            vmem_limit_bytes=vmem_bytes, collective_id=0, has_side_effects=True
        ),
    )(
        rep_weights,
        covariate_codes,
        tract_of.reshape(1, people),
        log_income.astype(f32).reshape(1, people),
        jnp.broadcast_to(controls[:, None], (size, reps)),
        threshold_grid.reshape(-1, lanes),
    )


def solution(mesh):
    placed = (
        P(None, ("rec", "tract")),
        P(None, ("rec", "tract")),
        P(("rec", "tract"), None),
        P(("rec", "tract")),
        P(),
        P(),
    )
    return jax.shard_map(
        shards,
        mesh=mesh,
        in_specs=placed,
        out_specs=(P(None, ("rec", "tract")), P("tract", None, "rec")),
        check_vma=False,
    )
```

```python
import functools

import jax
import jax.numpy as jnp
from jax import lax
from jax.experimental import pallas as pl
from jax.experimental.pallas import tpu as pltpu
from jax.sharding import PartitionSpec as P

smooth_width = 3.0 / 8192.0
grid_middle = 2048.0
grid_step = 3.0 / 2048.0
half_scale = 0.5 / smooth_width
base_levels = 16
first_kept = 4
kept = base_levels - first_kept
lanes = 128
bf16 = jnp.bfloat16
f32 = jnp.float32
vmem_bytes = 60 * 1024 * 1024


def firsts_of(variables):
    return [0] + [first_kept] * (variables - 1)


def pair_layout(variables):
    offsets, row = {}, 0
    for u, first in enumerate(firsts_of(variables)):
        for v in range(u + 1, variables):
            offsets[u, v] = row
            row += (base_levels - first) * kept
    return offsets, row, row + base_levels


def split3(value, axis):
    high = value.astype(bf16)
    rest = value - high.astype(f32)
    middle = rest.astype(bf16)
    low = (rest - middle.astype(f32)).astype(bf16)
    return jnp.concatenate([high, middle, low], axis=axis)


def one_hot(key, rows):
    row = lax.broadcasted_iota(jnp.int32, (rows, key.shape[1]), 0)
    return jnp.where(row == key, 1.0, 0.0).astype(bf16)


def remote(source, target, send_sem, recv_sem, where):
    return pltpu.make_async_remote_copy(
        src_ref=source,
        dst_ref=target,
        send_sem=send_sem,
        recv_sem=recv_sem,
        device_id=where,
        device_id_type=pl.DeviceIdType.MESH,
    )


def encode(value):
    top = jnp.max(jnp.max(jnp.abs(value), axis=0, keepdims=True), axis=1, keepdims=True)
    power = jnp.ceil(jnp.log2(jnp.maximum(top, 1e-30)))
    coded = jnp.round(value * (code_top * jnp.exp2(-power)))
    power = jnp.broadcast_to(power, (16, value.shape[1]))
    return jnp.concatenate([coded, power], axis=0).astype(jnp.int32).astype(jnp.int16)


def decode(coded):
    coded = coded.astype(jnp.int32).astype(f32)
    reps = coded.shape[0] - 16
    return coded[:reps] * (jnp.exp2(coded[reps : reps + 1]) * (1.0 / code_top))


def solve(variables, sums, aims, mat, rhs, coef, sol):
    size = mat.shape[0]
    offsets, singles, _ = pair_layout(variables)
    firsts = firsts_of(variables)
    starts = [0] + [base_levels + kept * (v - 1) for v in range(1, variables)]
    mat[...] = jnp.zeros_like(mat)
    for v in range(variables):
        count = base_levels - firsts[v]
        if v == 0:
            single = sums[singles : singles + count, :]
        else:
            at = offsets[0, v]
            single = sums[at : at + kept, :]
            for c in range(1, base_levels):
                single = single + sums[at + c * kept : at + (c + 1) * kept, :]
        rhs[starts[v] : starts[v] + count, :] = (
            aims[starts[v] : starts[v] + count, :] - single
        )
        for c in range(count):
            mat[starts[v] + c, starts[v] + c : starts[v] + c + 1, :] = single[c : c + 1, :]
    for (u, v), row in offsets.items():
        for c in range(base_levels - firsts[u]):
            at = row + c * kept
            mat[starts[u] + c, starts[v] : starts[v] + kept, :] = sums[at : at + kept, :]

    for block in range(size // 8):
        low = block * 8

        def eliminate(inner, carry, low=low, block=block):
            k = low + inner
            row = mat[k, low:, :]
            pivot = mat[k, pl.ds(k, 1), :]
            place = lax.broadcasted_iota(jnp.int32, row.shape, 0) + low
            factor = jnp.where(place > k, row * (1.0 / pivot), 0.0)
            coef[low:, :] = factor
            rhs[low:, :] = rhs[low:, :] - factor * rhs[pl.ds(k, 1), :]
            for other in range(block, size // 8):
                part = row[other * 8 - low :, :]
                for i in range(other * 8, other * 8 + 8):
                    mat[i, other * 8 :, :] = mat[i, other * 8 :, :] - coef[i : i + 1, :] * part
            return carry

        lax.fori_loop(0, 8, eliminate, 0)

    sol[...] = jnp.zeros_like(sol)
    for block in reversed(range(size // 8)):
        low = block * 8

        def substitute(inner, carry, low=low):
            k = low + 7 - inner
            known = jnp.sum(mat[k, low:, :] * sol[low:, :], axis=0, keepdims=True)
            sol[pl.ds(k, 1), :] = (rhs[pl.ds(k, 1), :] - known) / mat[k, pl.ds(k, 1), :]
            return carry

        lax.fori_loop(0, 8, substitute, 0)

    parts = []
    for v in range(variables):
        count = base_levels - firsts[v]
        if firsts[v]:
            parts.append(jnp.zeros((firsts[v], sol.shape[1]), f32))
        parts.append(sol[starts[v] : starts[v] + count, :])
    return jnp.concatenate(parts, axis=0)


gram_block = 1024
quarter = 1024
low_weight, high_weight = 0.5, 2.0
code_step = (high_weight - low_weight) / 65535.0
code_top = 32000.0


def kernel(
    ny, tracts, nx,
    w_ref, codes_ref, tract_ref, income_ref, controls_ref, grid_ref,
    cal_ref, tab_ref,
    pieces, pairs, acc, gram, from_sister, from_chip, final, sums, mat, rhs, coef, sol, x3,
    about, coded, others, located, corner, cen, smooth, design, sent, masked, masked_too, table,
    to_x, from_x, over_x, to_z, from_z,
    about_sems, other_sems, sister_sems, send_chip, recv_chip, send_back, recv_back,
    final_sems, x_sems, z_sems,
):
    reps, people = w_ref.shape
    variables = codes_ref.shape[0]
    nz = tracts // nx
    blocks = 2 * ny
    chips = ny * tracts
    half = reps // 2
    tiles = gram.shape[1]
    offsets, singles, rows = pair_layout(variables)
    firsts = firsts_of(variables)
    share = smooth.shape[1]
    pieces_j = share // lanes
    quarters = people // quarter

    rec, tract = lax.axis_index("rec"), lax.axis_index("tract")
    y, core = lax.div(rec, 2), lax.rem(rec, 2)
    z, x = lax.div(tract, nx), lax.rem(tract, nx)
    sister = {"rec": 2 * y + 1 - core}
    shift = tracts - 2
    chip = y * tracts + lax.rem(tract + shift, tracts)

    def chip_at(number):
        return {
            "rec": 2 * lax.div(number, tracts) + core,
            "tract": lax.rem(lax.rem(number, tracts) + tracts - shift, tracts),
        }

    def each_other(count, body):
        def step(d, carry):
            body(lax.rem(chip + d, count))
            return carry

        lax.fori_loop(1, count, step, 0)

    barrier = pltpu.get_barrier_semaphore()
    pl.semaphore_signal(barrier, inc=1, device_id=sister, device_id_type=pl.DeviceIdType.MESH)
    each_other(
        chips,
        lambda peer: pl.semaphore_signal(
            barrier, inc=1, device_id=chip_at(peer), device_id_type=pl.DeviceIdType.MESH
        ),
    )

    income = income_ref[...].astype(f32)
    for q in range(quarters):
        cols = slice(q * quarter, (q + 1) * quarter)
        located[q, 0:variables, :] = codes_ref[:, cols].astype(f32)
        located[q, variables : variables + 1, :] = tract_ref[:, cols].astype(f32)
        for i in range(quarter // lanes):
            row = q * (quarter // lanes) + i
            located[q, variables + 1 : variables + 2, i * lanes : (i + 1) * lanes] = income[
                row : row + 1, :
            ]
        located[q, variables + 2 :, :] = jnp.zeros(
            (located.shape[1] - variables - 2, quarter), f32
        )
    for q in range(quarters // 2):
        about[0, :, q * quarter : (q + 1) * quarter] = jnp.concatenate(
            [located[q], located[quarters // 2 + q]], axis=0
        ).astype(bf16)
    for q in range(quarters):
        part = w_ref[:, q * quarter : (q + 1) * quarter]
        coded[q] = jnp.round((part - low_weight) / code_step - 32768.0).astype(jnp.int32).astype(jnp.int16)
    pieces[...] = split3(w_ref[...], 0)

    def spread(source, slot, sems):
        return [remote(source, slot(1), sems.at[0, 1], sems.at[1, 1], sister)] + [
            remote(
                source,
                slot(2 * e),
                sems.at[0, 2 * e],
                sems.at[1, 2 * e],
                {"rec": 2 * lax.rem(y - e + ny, ny) + core},
            )
            for e in range(1, ny)
        ]

    def relay(slot, sems):
        return [
            remote(
                slot(2 * e), slot(2 * e + 1), sems.at[0, 2 * e + 1], sems.at[1, 2 * e + 1], sister
            )
            for e in range(1, ny)
        ]

    about_slot = lambda b: about.at[b]
    def other_slot(q):
        return lambda b: others.at[b - 1, q]

    about_copies = spread(about.at[0], about_slot, about_sems)
    other_copies = [
        spread(coded.at[q], other_slot(q), other_sems.at[q]) for q in range(quarters)
    ]
    about_relay = relay(about_slot, about_sems)
    other_relay = [relay(other_slot(q), other_sems.at[q]) for q in range(quarters)]
    def start_over_y(first, last):
        for q in range(first, last):
            for copy in other_copies[q][1:]:
                copy.start()


    cut = offsets[1, 2] // lanes
    chunks = [(0, cut), (cut, tiles)]

    def gram_chunk(first, last):
        low, high = first * lanes, last * lanes
        groups = []
        for (u, v), row in offsets.items():
            if low <= row < high:
                groups.append((u, v, row - low, (base_levels - firsts[u]) * kept))
        acc[:, : high - low] = jnp.zeros((acc.shape[0], high - low), f32)

        def body(i, carry):
            cols = pl.ds(pl.multiple_of(i * gram_block, gram_block), gram_block)
            for u, v, row, count in groups:
                right = codes_ref[v : v + 1, cols] - first_kept
                key = (codes_ref[u : u + 1, cols] - firsts[u]) * kept + right
                key = jnp.where(right < 0, -1, key)
                pairs[row : row + count, :] = one_hot(key, count)
            if low <= singles < high:
                pairs[singles - low : high - low, :] = one_hot(
                    codes_ref[0:1, cols], high - singles
                )
            acc[:, : high - low] += lax.dot_general(
                pieces[:, cols],
                pairs[: high - low, :],
                (((1,), (1,)), ((), ())),
                preferred_element_type=f32,
            )
            return carry

        lax.fori_loop(0, people // gram_block, body, 0)
        for t in range(first, last):
            at = slice((t - first) * lanes, (t - first + 1) * lanes)
            value = acc[:reps, at] + acc[reps : 2 * reps, at] + acc[2 * reps :, at]
            gram[0, t] = value[:half]
            gram[1, t] = value[half:]

    def to_sister(c):
        first, last = chunks[c]
        return remote(
            gram.at[1 - core, first:last],
            from_sister.at[first:last],
            sister_sems.at[0, c],
            sister_sems.at[1, c],
            sister,
        )

    def to_chips(c):
        first, last = chunks[c]
        to_sister(c).wait_recv()
        for t in range(first, last):
            gram[core, t] = gram[core, t] + from_sister[t]

        def start(peer):
            @pl.when((peer >= first) & (peer < last))
            def _():
                remote(
                    gram.at[core, peer],
                    from_chip.at[chip],
                    send_chip.at[peer],
                    recv_chip.at[chip],
                    chip_at(peer),
                ).start()

        each_other(chips, start)

    def smooth_part(b):
        if b > 0:
            for q in range(quarters // 2):
                value = about[b, :, q * quarter : (q + 1) * quarter].astype(f32)
                located[b * quarters + q] = value[:8]
                located[b * quarters + quarters // 2 + q] = value[8:]

        def body(q, carry):
            c = b * quarters + q
            income = located[c, variables + 1 : variables + 2, :] * half_scale
            for i in range(quarter // lanes):
                at = slice(i * lanes, (i + 1) * lanes)
                smooth[c, :, at] = (0.5 + 0.5 * jnp.tanh(cen[...] - income[:, at])).astype(bf16)
            for v in range(variables):
                code = located[c, v : v + 1, :].astype(jnp.int32)
                design[c, v * base_levels : (v + 1) * base_levels, :] = one_hot(code, base_levels)
            return carry

        lax.fori_loop(0, quarters, body, 0)

    gram_chunk(*chunks[0])
    gram_chunk(*chunks[1])
    pl.semaphore_wait(barrier, chips)
    to_sister(0).start()
    to_sister(1).start()
    for copy in about_copies[1:] + about_copies[:1]:
        copy.start()
    start_over_y(0, quarters // 2)
    to_chips(0)

    corner[...] = jnp.zeros_like(corner)
    count = share // lanes
    corner[:count, :] = (
        (grid_ref[pl.ds(rec * count, count), :].astype(f32) - grid_middle)
        * (grid_step * half_scale)
    )
    corner[count : count + 1, : controls_ref.shape[1]] = controls_ref[...]
    turned = corner[...].T
    for i in range(count):
        cen[i * lanes : (i + 1) * lanes, :] = jnp.broadcast_to(turned[:, i : i + 1], (lanes, lanes))

    size = mat.shape[0]
    aims = jnp.broadcast_to(turned[:size, count : count + 1], (size, reps))
    to_chips(1)
    start_over_y(quarters // 2, quarters - 1)
    for q in range(quarters):
        other_copies[q][0].start()
    smooth_part(0)
    for e in range(1, ny):
        about_copies[e].wait_recv()
        about_relay[e - 1].start()

    @pl.when(chip < tiles)
    def _():
        each_other(
            chips,
            lambda peer: remote(
                gram.at[core, 0], from_chip.at[peer], send_chip.at[0], recv_chip.at[peer], sister
            ).wait_recv(),
        )
        total = lax.fori_loop(
            1,
            chips,
            lambda d, value: value + from_chip[lax.rem(chip + d, chips)],
            gram[core, chip],
        )
        final[core, chip] = total
        each_other(
            chips,
            lambda peer: remote(
                final.at[core, chip],
                final.at[core, chip],
                send_back.at[peer],
                recv_back.at[chip],
                chip_at(peer),
            ).start(),
        )

    about_copies[0].wait_recv()
    smooth_part(1)

    def hand_over(t):
        return remote(
            final.at[core, t], final.at[core, t], final_sems.at[0, t], final_sems.at[1, t], sister
        )

    def taken(t):
        return remote(
            final.at[core, t],
            final.at[1 - core, t],
            final_sems.at[0, t],
            final_sems.at[1, t],
            sister,
        )

    for t in range(tiles):
        @pl.when(chip != t)
        def _():
            remote(
                final.at[core, t], final.at[core, t], send_back.at[0], recv_back.at[t], sister
            ).wait_recv()

        hand_over(t).start()
    start_over_y(quarters - 1, quarters)
    for e in range(1, ny):
        smooth_part(2 * e)
        about_relay[e - 1].wait_recv()
        smooth_part(2 * e + 1)
    for t in range(tiles):
        taken(t).wait_recv()
        whole = jnp.concatenate([final[0, t], final[1, t]], axis=0)
        sums[t * lanes : (t + 1) * lanes, :] = whole.T

    def relay_over_y(first, last):
        for q in range(first, last):
            for e in range(1, ny):
                other_copies[q][e].wait_recv()
                other_relay[q][e - 1].start()

    relay_over_y(0, quarters // 2)
    x3[...] = split3(solve(variables, sums, aims, mat, rhs, coef, sol), 0)
    relay_over_y(quarters // 2, quarters)

    def factors(c):
        return 1.0 + lax.dot_general(
            x3[...],
            jnp.concatenate([design[c]] * 3, axis=0),
            (((0,), (0,)), ((), ())),
            preferred_element_type=f32,
        )

    def own_weights(q, carry):
        cols = pl.ds(pl.multiple_of(q * quarter, quarter), quarter)
        factor = factors(q)
        cal_ref[:, cols] = factor
        sent[q] = (w_ref[:, cols] * factor).astype(bf16)
        return carry

    lax.fori_loop(0, quarters, own_weights, 0)

    def other_weights(b, q):
        code = others[b - 1, q].astype(jnp.int32).astype(f32)
        weights = (code + 32768.0) * code_step + low_weight
        sent[b * quarters + q] = (weights * factors(b * quarters + q)).astype(bf16)

    halves = pieces_j // 2

    def mask(c, e, target):
        own = located[c, variables : variables + 1, :]
        value = sent[c]
        for k in range(nz):
            place = (k * nx + lax.rem(x + e, nx)).astype(f32)
            inside = jnp.where(own == place, 1.0, 0.0).astype(bf16)
            target[k * reps : (k + 1) * reps, :] = value * inside

    def add_product(c, source, e, first, count):
        product = lax.dot_general(
            source[...],
            smooth[c, first * lanes : (first + count) * lanes, :],
            (((1,), (1,)), ((), ())),
            preferred_element_type=f32,
        )
        for j in range(count):
            table[e, first + j] += product[:, j * lanes : (j + 1) * lanes]

    last = blocks * quarters - 1

    def table_loop(e, first, count, low, high, b=None):
        def body(i, carry):
            c = 2 * i
            add_product(c, masked, e, first, count)
            mask(c + 1, e, masked_too)
            if b is not None:
                other_weights(b, c - (b - 1) * quarters)
            add_product(c + 1, masked_too, e, first, count)
            if b is not None:
                other_weights(b, c + 1 - (b - 1) * quarters)
            mask(jnp.minimum(c + 2, last), e, masked)
            return carry

        lax.fori_loop(low // 2, high // 2, body, 0)

    def across_x(e, j):
        return remote(
            to_x.at[e - 1, j],
            from_x.at[e - 1, j],
            x_sems.at[0, e - 1, j],
            x_sems.at[1, e - 1, j],
            {"tract": z * nx + lax.rem(x + e, nx)},
        )

    def along_z(e, j):
        return remote(
            to_z.at[e - 1, j],
            from_z.at[e - 1, j],
            z_sems.at[0, e - 1, j],
            z_sems.at[1, e - 1, j],
            {"tract": lax.rem(z + e, nz) * nx + x},
        )

    def send_over_x(e, part):
        for j in range(part * halves, (part + 1) * halves):
            for k in range(nz):
                to_x[e - 1, j, k] = encode(table[e, j, k * reps : (k + 1) * reps, :])
            across_x(e, j).start()

    def send_along_z(part):
        for j in range(part * halves, (part + 1) * halves):
            for e in range(1, nx):
                across_x(e, j).wait_recv()
            for k in range(nz):
                value = table[0, j, k * reps : (k + 1) * reps, :]
                for e in range(1, nx):
                    value = value + decode(from_x[e - 1, j, k])
                over_x[j, k] = value
            for e in range(1, nz):
                to_z[e - 1, j] = encode(over_x[j, lax.rem(z + e, nz)])
                along_z(e, j).start()

    table[...] = jnp.zeros_like(table)
    for e in range(1, nx):
        for part in range(2):
            mask(0, e, masked)
            if e > 1 or part > 0:
                table_loop(e, part * halves, halves, 0, blocks * quarters)
            else:
                for b in range(blocks):
                    if b + 1 < blocks and (b + 1) % 2 == 1:
                        for q in range(quarters):
                            arrived = other_copies[q][0] if b == 0 else other_relay[q][b // 2 - 1]
                            arrived.wait_recv()
                    following = b + 1 if b + 1 < blocks else None
                    table_loop(e, 0, halves, b * quarters, (b + 1) * quarters, following)
            send_over_x(e, part)
    for part in range(2):
        mask(0, 0, masked)
        table_loop(0, part * halves, halves, 0, blocks * quarters)
        send_along_z(part)
    for j in range(pieces_j):
        value = over_x[j, z]
        for e in range(1, nz):
            along_z(e, j).wait_recv()
            value = value + decode(from_z[e - 1, j])
        tab_ref[0, :, j * lanes : (j + 1) * lanes] = value

    for copy in about_copies + about_relay + sum(other_copies + other_relay, []):
        copy.wait_send()
    for c in range(2):
        to_sister(c).wait_send()

    def left(peer):
        @pl.when(peer < tiles)
        def _():
            remote(
                gram.at[core, peer], from_chip.at[chip], send_chip.at[peer], recv_chip.at[chip],
                chip_at(peer),
            ).wait_send()

        @pl.when(chip < tiles)
        def _():
            remote(
                final.at[core, chip], final.at[core, chip], send_back.at[peer], recv_back.at[chip],
                chip_at(peer),
            ).wait_send()

    each_other(chips, left)
    for t in range(tiles):
        hand_over(t).wait_send()
    for j in range(pieces_j):
        for e in range(1, nx):
            across_x(e, j).wait_send()
        for e in range(1, nz):
            along_z(e, j).wait_send()


def shards(rep_weights, covariate_codes, tract_of, log_income, controls, threshold_grid):
    reps, people = rep_weights.shape
    variables = covariate_codes.shape[0]
    tracts = lax.axis_size("tract")
    recs = lax.axis_size("rec")
    ny = recs // 2
    nz = 4
    nx = tracts // nz
    chips = ny * tracts
    share = threshold_grid.shape[0] // recs
    pieces_j = share // lanes
    quarters = people // quarter
    size = controls.shape[0]
    rows = pair_layout(variables)[2]
    tiles = -(-rows // lanes)
    cut = pair_layout(variables)[0][1, 2] // lanes
    most = max(cut, tiles - cut) * lanes
    designs = variables * base_levels
    vmem = pltpu.VMEM
    dma = pltpu.SemaphoreType.DMA
    factor, tables = pl.pallas_call(
        functools.partial(kernel, ny, tracts, nx),
        in_specs=[pl.BlockSpec(memory_space=vmem)] * 6,
        out_specs=[pl.BlockSpec(memory_space=vmem)] * 2,
        out_shape=[
            jax.ShapeDtypeStruct((reps, people), f32),
            jax.ShapeDtypeStruct((1, reps, share), f32),
        ],
        scratch_shapes=[
            vmem((3 * reps, people), bf16),
            vmem((most, gram_block), bf16),
            vmem((3 * reps, most), f32),
            vmem((2, tiles, reps // 2, lanes), f32),
            vmem((tiles, reps // 2, lanes), f32),
            vmem((chips, reps // 2, lanes), f32),
            vmem((2, tiles, reps // 2, lanes), f32),
            vmem((tiles * lanes, reps), f32),
            vmem((size, size, reps), f32),
            vmem((size, reps), f32),
            vmem((size, reps), f32),
            vmem((size, reps), f32),
            vmem((3 * designs, reps), bf16),
            vmem((recs, 16, people // 2), bf16),
            vmem((people // quarter, reps, quarter), jnp.int16),
            vmem((recs - 1, people // quarter, reps, quarter), jnp.int16),
            vmem((recs * quarters, 8, quarter), f32),
            vmem((8, lanes), f32),
            vmem((share, lanes), f32),
            vmem((recs * quarters, share, quarter), bf16),
            vmem((recs * quarters, designs, quarter), bf16),
            vmem((recs * quarters, reps, quarter), bf16),
            vmem((nz * reps, quarter), bf16),
            vmem((nz * reps, quarter), bf16),
            vmem((nx, pieces_j, nz * reps, lanes), f32),
            vmem((nx - 1, pieces_j, nz, reps + 16, lanes), jnp.int16),
            vmem((nx - 1, pieces_j, nz, reps + 16, lanes), jnp.int16),
            vmem((pieces_j, nz, reps, lanes), f32),
            vmem((nz - 1, pieces_j, reps + 16, lanes), jnp.int16),
            vmem((nz - 1, pieces_j, reps + 16, lanes), jnp.int16),
            dma((2, recs)),
            dma((people // quarter, 2, recs)),
            dma((2, 2)),
            dma((tiles,)),
            dma((chips,)),
            dma((chips,)),
            dma((tiles,)),
            dma((2, tiles)),
            dma((2, nx - 1, pieces_j)),
            dma((2, nz - 1, pieces_j)),
        ],
        compiler_params=pltpu.CompilerParams(
            vmem_limit_bytes=vmem_bytes, collective_id=0, has_side_effects=True
        ),
    )(
        rep_weights,
        covariate_codes,
        tract_of.reshape(1, people),
        log_income.reshape(-1, lanes),
        controls.reshape(1, size),
        threshold_grid.reshape(-1, lanes),
    )
    return rep_weights * factor, tables / float(people * recs)


def solution(mesh):
    placed = (
        P(None, ("rec", "tract")),
        P(None, ("rec", "tract")),
        P(("rec", "tract"), None),
        P(("rec", "tract")),
        P(),
        P(),
    )
    return jax.shard_map(
        shards,
        mesh=mesh,
        in_specs=placed,
        out_specs=(P(None, ("rec", "tract")), P("tract", None, "rec")),
        check_vma=False,
    )
```

```python
import functools

import jax
import jax.numpy as jnp
from jax import lax
from jax.experimental import pallas as pl
from jax.experimental.pallas import tpu as pltpu
from jax.sharding import PartitionSpec as P

smooth_width = 3.0 / 8192.0
grid_middle = 2048.0
grid_step = 3.0 / 2048.0
half_scale = 0.5 / smooth_width
base_levels = 16
first_kept = 4
kept = base_levels - first_kept
lanes = 128
bf16 = jnp.bfloat16
f32 = jnp.float32
vmem_bytes = 60 * 1024 * 1024


def firsts_of(variables):
    return [0] + [first_kept] * (variables - 1)


def pair_layout(variables):
    offsets, row = {}, 0
    for u, first in enumerate(firsts_of(variables)):
        for v in range(u + 1, variables):
            offsets[u, v] = row
            row += (base_levels - first) * kept
    return offsets, row, row + base_levels


def split3(value, axis):
    high = value.astype(bf16)
    rest = value - high.astype(f32)
    middle = rest.astype(bf16)
    low = (rest - middle.astype(f32)).astype(bf16)
    return jnp.concatenate([high, middle, low], axis=axis)


def one_hot(key, rows):
    row = lax.broadcasted_iota(jnp.int32, (rows, key.shape[1]), 0)
    return jnp.where(row == key, 1.0, 0.0).astype(bf16)


def remote(source, target, send_sem, recv_sem, where):
    return pltpu.make_async_remote_copy(
        src_ref=source,
        dst_ref=target,
        send_sem=send_sem,
        recv_sem=recv_sem,
        device_id=where,
        device_id_type=pl.DeviceIdType.MESH,
    )


def encode(value):
    top = jnp.max(jnp.max(jnp.abs(value), axis=0, keepdims=True), axis=1, keepdims=True)
    power = jnp.ceil(jnp.log2(jnp.maximum(top, 1e-30)))
    coded = jnp.round(value * (code_top * jnp.exp2(-power)))
    power = jnp.broadcast_to(power, (16, value.shape[1]))
    return jnp.concatenate([coded, power], axis=0).astype(jnp.int32).astype(jnp.int16)


def decode(coded):
    coded = coded.astype(jnp.int32).astype(f32)
    reps = coded.shape[0] - 16
    return coded[:reps] * (jnp.exp2(coded[reps : reps + 1]) * (1.0 / code_top))


def solve(variables, sums, aims, mat, rhs, coef, sol):
    size = mat.shape[0]
    offsets, singles, _ = pair_layout(variables)
    firsts = firsts_of(variables)
    starts = [0] + [base_levels + kept * (v - 1) for v in range(1, variables)]
    mat[...] = jnp.zeros_like(mat)
    for v in range(variables):
        count = base_levels - firsts[v]
        if v == 0:
            single = sums[singles : singles + count, :]
        else:
            at = offsets[0, v]
            single = sums[at : at + kept, :]
            for c in range(1, base_levels):
                single = single + sums[at + c * kept : at + (c + 1) * kept, :]
        rhs[starts[v] : starts[v] + count, :] = (
            aims[starts[v] : starts[v] + count, :] - single
        )
        for c in range(count):
            mat[starts[v] + c, starts[v] + c : starts[v] + c + 1, :] = single[c : c + 1, :]
    for (u, v), row in offsets.items():
        for c in range(base_levels - firsts[u]):
            at = row + c * kept
            mat[starts[u] + c, starts[v] : starts[v] + kept, :] = sums[at : at + kept, :]

    inverses = []
    for low in range(0, size, 8):
        rows = [mat[low + p, low:, :] for p in range(8)]
        right = rhs[low:, :]
        place = lax.broadcasted_iota(jnp.int32, rows[0].shape, 0)
        for p in range(8):
            inverse = 1.0 / rows[p][p : p + 1, :]
            factor = jnp.where(place > p, rows[p] * inverse, 0.0)
            coef[p, low:, :] = factor
            for q in range(p + 1, 8):
                rows[q] = rows[q] - factor[q : q + 1, :] * rows[p]
            right = right - factor * right[p : p + 1, :]
            inverses.append(inverse)
        rhs[low:, :] = right
        for p in range(8):
            mat[low + p, low:, :] = rows[p]
        for other in range(low + 8, size, 8):

            def update(pair, carry, low=low, other=other):
                for i in (other + 2 * pair, other + 2 * pair + 1):
                    value = mat[i, other:, :]
                    for p in range(8):
                        value = value - coef[p, pl.ds(i, 1), :] * mat[low + p, other:, :]
                    mat[i, other:, :] = value
                return carry

            lax.fori_loop(0, 4, update, 0)

    for low in reversed(range(0, size, 8)):
        known = []
        for p in range(8):
            value = rhs[low + p : low + p + 1, :]
            if low + 8 < size:
                later = mat[low + p, low + 8 :, :] * sol[low + 8 :, :]
                value = value - jnp.sum(later, axis=0, keepdims=True)
            known.append(value)
        for p in reversed(range(8)):
            found = known[p] * inverses[low + p]
            sol[low + p : low + p + 1, :] = found
            for q in range(p):
                known[q] = known[q] - mat[low + q, low + p : low + p + 1, :] * found

    parts = []
    for v in range(variables):
        count = base_levels - firsts[v]
        if firsts[v]:
            parts.append(jnp.zeros((firsts[v], sol.shape[1]), f32))
        parts.append(sol[starts[v] : starts[v] + count, :])
    return jnp.concatenate(parts, axis=0)


gram_block = 1024
quarter = 1024
low_weight, high_weight = 0.5, 2.0
code_step = (high_weight - low_weight) / 65535.0
code_top = 32000.0


def kernel(
    ny, tracts, nx, scale,
    w_hbm, codes_ref, tract_ref, income_ref, controls_ref, grid_ref,
    cal_hbm, tab_hbm,
    w_ref, tab_ref, w_sems, cal_sem, tab_sem,
    pieces, pairs, acc, gram, from_sister, from_chip, final, sums, mat, rhs, coef, sol, x3,
    about, coded, others, located, corner, cen, smooth, design, sent, masked, masked_too, table,
    to_x, from_x, over_x, to_z, from_z,
    about_sems, other_sems, sister_sems, send_chip, recv_chip, send_back, recv_back,
    final_sems, x_sems, z_sems,
):
    reps, people = w_ref.shape
    variables = codes_ref.shape[0]
    quarters = people // quarter
    nz = tracts // nx
    blocks = 2 * ny
    chips = ny * tracts
    half = reps // 2
    tiles = gram.shape[1]
    offsets, singles, rows = pair_layout(variables)
    firsts = firsts_of(variables)
    share = smooth.shape[1]
    pieces_j = share // lanes

    loads = [
        pltpu.make_async_copy(
            w_hbm.at[:, q * quarter : (q + 1) * quarter],
            w_ref.at[:, q * quarter : (q + 1) * quarter],
            w_sems.at[q],
        )
        for q in range(quarters)
    ]
    for load in loads:
        load.start()

    rec, tract = lax.axis_index("rec"), lax.axis_index("tract")
    y, core = lax.div(rec, 2), lax.rem(rec, 2)
    z, x = lax.div(tract, nx), lax.rem(tract, nx)
    sister = {"rec": 2 * y + 1 - core}
    shift = tracts - 2
    chip = y * tracts + lax.rem(tract + shift, tracts)

    def chip_at(number):
        return {
            "rec": 2 * lax.div(number, tracts) + core,
            "tract": lax.rem(lax.rem(number, tracts) + tracts - shift, tracts),
        }

    def each_other(count, body):
        def step(d, carry):
            body(lax.rem(chip + d, count))
            return carry

        lax.fori_loop(1, count, step, 0)

    barrier = pltpu.get_barrier_semaphore()
    pl.semaphore_signal(barrier, inc=1, device_id=sister, device_id_type=pl.DeviceIdType.MESH)
    each_other(
        chips,
        lambda peer: pl.semaphore_signal(
            barrier, inc=1, device_id=chip_at(peer), device_id_type=pl.DeviceIdType.MESH
        ),
    )

    income = income_ref[...].astype(f32)
    for q in range(quarters):
        cols = slice(q * quarter, (q + 1) * quarter)
        located[q, 0:variables, :] = codes_ref[:, cols].astype(f32)
        located[q, variables : variables + 1, :] = tract_ref[:, cols].astype(f32)
        for i in range(quarter // lanes):
            row = q * (quarter // lanes) + i
            located[q, variables + 1 : variables + 2, i * lanes : (i + 1) * lanes] = income[
                row : row + 1, :
            ]
        located[q, variables + 2 :, :] = jnp.zeros(
            (located.shape[1] - variables - 2, quarter), f32
        )
    for q in range(quarters // 2):
        about[0, :, q * quarter : (q + 1) * quarter] = jnp.concatenate(
            [located[q], located[quarters // 2 + q]], axis=0
        ).astype(bf16)
    for q in range(quarters):
        loads[q].wait()
        part = w_ref[:, q * quarter : (q + 1) * quarter]
        coded[q] = jnp.round((part - low_weight) / code_step - 32768.0).astype(jnp.int32).astype(jnp.int16)
    pieces[...] = split3(w_ref[...], 0)

    def spread(source, slot, sems):
        return [remote(source, slot(1), sems.at[0, 1], sems.at[1, 1], sister)] + [
            remote(
                source,
                slot(2 * e),
                sems.at[0, 2 * e],
                sems.at[1, 2 * e],
                {"rec": 2 * lax.rem(y - e + ny, ny) + core},
            )
            for e in range(1, ny)
        ]

    def relay(slot, sems):
        return [
            remote(
                slot(2 * e), slot(2 * e + 1), sems.at[0, 2 * e + 1], sems.at[1, 2 * e + 1], sister
            )
            for e in range(1, ny)
        ]

    about_slot = lambda b: about.at[b]
    def other_slot(q):
        return lambda b: others.at[b - 1, q]

    about_copies = spread(about.at[0], about_slot, about_sems)
    other_copies = [
        spread(coded.at[q], other_slot(q), other_sems.at[q]) for q in range(quarters)
    ]
    about_relay = relay(about_slot, about_sems)
    other_relay = [relay(other_slot(q), other_sems.at[q]) for q in range(quarters)]
    def start_over_y(first, last):
        for q in range(first, last):
            for copy in other_copies[q][1:]:
                copy.start()


    cut = offsets[1, 2] // lanes
    chunks = [(0, cut), (cut, tiles)]

    def gram_chunk(first, last):
        low, high = first * lanes, last * lanes
        groups = []
        for (u, v), row in offsets.items():
            if low <= row < high:
                groups.append((u, v, row - low, (base_levels - firsts[u]) * kept))
        acc[:, : high - low] = jnp.zeros((acc.shape[0], high - low), f32)

        def body(i, carry):
            cols = pl.ds(pl.multiple_of(i * gram_block, gram_block), gram_block)
            for u, v, row, count in groups:
                right = codes_ref[v : v + 1, cols] - first_kept
                key = (codes_ref[u : u + 1, cols] - firsts[u]) * kept + right
                key = jnp.where(right < 0, -1, key)
                pairs[row : row + count, :] = one_hot(key, count)
            if low <= singles < high:
                pairs[singles - low : high - low, :] = one_hot(
                    codes_ref[0:1, cols], high - singles
                )
            acc[:, : high - low] += lax.dot_general(
                pieces[:, cols],
                pairs[: high - low, :],
                (((1,), (1,)), ((), ())),
                preferred_element_type=f32,
            )
            return carry

        lax.fori_loop(0, people // gram_block, body, 0)
        for t in range(first, last):
            at = slice((t - first) * lanes, (t - first + 1) * lanes)
            value = acc[:reps, at] + acc[reps : 2 * reps, at] + acc[2 * reps :, at]
            gram[0, t] = value[:half]
            gram[1, t] = value[half:]

    def to_sister(c):
        first, last = chunks[c]
        return remote(
            gram.at[1 - core, first:last],
            from_sister.at[first:last],
            sister_sems.at[0, c],
            sister_sems.at[1, c],
            sister,
        )

    def to_chips(c):
        first, last = chunks[c]
        to_sister(c).wait_recv()
        for t in range(first, last):
            gram[core, t] = gram[core, t] + from_sister[t]

        def start(peer):
            @pl.when((peer >= first) & (peer < last))
            def _():
                remote(
                    gram.at[core, peer],
                    from_chip.at[chip],
                    send_chip.at[peer],
                    recv_chip.at[chip],
                    chip_at(peer),
                ).start()

        each_other(chips, start)

    def smooth_part(b):
        if b > 0:
            for q in range(quarters // 2):
                value = about[b, :, q * quarter : (q + 1) * quarter].astype(f32)
                located[b * quarters + q] = value[:8]
                located[b * quarters + quarters // 2 + q] = value[8:]

        def body(q, carry):
            c = b * quarters + q
            income = located[c, variables + 1 : variables + 2, :] * half_scale
            for i in range(quarter // lanes):
                at = slice(i * lanes, (i + 1) * lanes)
                smooth[c, :, at] = (0.5 + 0.5 * jnp.tanh(cen[...] - income[:, at])).astype(bf16)
            for v in range(variables):
                code = located[c, v : v + 1, :].astype(jnp.int32)
                design[c, v * base_levels : (v + 1) * base_levels, :] = one_hot(code, base_levels)
            return carry

        lax.fori_loop(0, quarters, body, 0)

    gram_chunk(*chunks[0])
    gram_chunk(*chunks[1])
    pl.semaphore_wait(barrier, chips)
    to_sister(0).start()
    to_sister(1).start()
    for copy in about_copies[1:] + about_copies[:1]:
        copy.start()
    start_over_y(0, 1)
    to_chips(0)

    corner[...] = jnp.zeros_like(corner)
    count = share // lanes
    corner[:count, :] = (
        (grid_ref[pl.ds(rec * count, count), :].astype(f32) - grid_middle)
        * (grid_step * half_scale)
    )
    corner[count : count + 1, : controls_ref.shape[1]] = controls_ref[...]
    turned = corner[...].T
    for i in range(count):
        cen[i * lanes : (i + 1) * lanes, :] = jnp.broadcast_to(turned[:, i : i + 1], (lanes, lanes))

    size = mat.shape[0]
    aims = jnp.broadcast_to(turned[:size, count : count + 1], (size, reps))
    to_chips(1)
    start_over_y(1, quarters // 2)
    smooth_part(0)
    for e in range(1, ny):
        about_copies[e].wait_recv()
        about_relay[e - 1].start()

    @pl.when(chip < tiles)
    def _():
        each_other(
            chips,
            lambda peer: remote(
                gram.at[core, 0], from_chip.at[peer], send_chip.at[0], recv_chip.at[peer], sister
            ).wait_recv(),
        )
        total = lax.fori_loop(
            1,
            chips,
            lambda d, value: value + from_chip[lax.rem(chip + d, chips)],
            gram[core, chip],
        )
        final[core, chip] = total
        each_other(
            chips,
            lambda peer: remote(
                final.at[core, chip],
                final.at[core, chip],
                send_back.at[peer],
                recv_back.at[chip],
                chip_at(peer),
            ).start(),
        )

    about_copies[0].wait_recv()
    smooth_part(1)

    def hand_over(t):
        return remote(
            final.at[core, t], final.at[core, t], final_sems.at[0, t], final_sems.at[1, t], sister
        )

    def taken(t):
        return remote(
            final.at[core, t],
            final.at[1 - core, t],
            final_sems.at[0, t],
            final_sems.at[1, t],
            sister,
        )

    for t in range(tiles):
        @pl.when(chip != t)
        def _():
            remote(
                final.at[core, t], final.at[core, t], send_back.at[0], recv_back.at[t], sister
            ).wait_recv()

        hand_over(t).start()
    start_over_y(quarters // 2, quarters)
    for q in range(quarters):
        other_copies[q][0].start()
    for e in range(1, ny):
        smooth_part(2 * e)
        about_relay[e - 1].wait_recv()
        smooth_part(2 * e + 1)
    for t in range(tiles):
        taken(t).wait_recv()
        whole = jnp.concatenate([final[0, t], final[1, t]], axis=0)
        sums[t * lanes : (t + 1) * lanes, :] = whole.T

    def relay_over_y(first, last):
        for q in range(first, last):
            for e in range(1, ny):
                other_copies[q][e].wait_recv()
                other_relay[q][e - 1].start()

    relay_over_y(0, quarters // 2)
    x3[...] = split3(solve(variables, sums, aims, mat, rhs, coef, sol), 0)
    relay_over_y(quarters // 2, quarters)

    def factors(c):
        return 1.0 + lax.dot_general(
            x3[...],
            jnp.concatenate([design[c]] * 3, axis=0),
            (((0,), (0,)), ((), ())),
            preferred_element_type=f32,
        )

    def own_weights(q, carry):
        cols = pl.ds(pl.multiple_of(q * quarter, quarter), quarter)
        calibrated = w_ref[:, cols] * factors(q)
        w_ref[:, cols] = calibrated
        sent[q] = calibrated.astype(bf16)
        return carry

    lax.fori_loop(0, quarters, own_weights, 0)
    cal_copy = pltpu.make_async_copy(w_ref, cal_hbm, cal_sem)
    cal_copy.start()

    def other_weights(b, q):
        code = others[b - 1, q].astype(jnp.int32).astype(f32)
        weights = (code + 32768.0) * code_step + low_weight
        sent[b * quarters + q] = (weights * factors(b * quarters + q)).astype(bf16)

    halves = pieces_j // 2

    def mask(c, e, target):
        own = located[c, variables : variables + 1, :]
        value = sent[c]
        for k in range(nz):
            place = (k * nx + lax.rem(x + e, nx)).astype(f32)
            inside = jnp.where(own == place, 1.0, 0.0).astype(bf16)
            target[k * reps : (k + 1) * reps, :] = value * inside

    def add_product(c, source, e, first, count):
        product = lax.dot_general(
            source[...],
            smooth[c, first * lanes : (first + count) * lanes, :],
            (((1,), (1,)), ((), ())),
            preferred_element_type=f32,
        )
        for j in range(count):
            table[e, first + j] += product[:, j * lanes : (j + 1) * lanes]

    last = blocks * quarters - 1

    def table_loop(e, first, count, low, high, b=None):
        def body(i, carry):
            c = 2 * i
            add_product(c, masked, e, first, count)
            mask(c + 1, e, masked_too)
            if b is not None:
                other_weights(b, c - (b - 1) * quarters)
            add_product(c + 1, masked_too, e, first, count)
            if b is not None:
                other_weights(b, c + 1 - (b - 1) * quarters)
            mask(jnp.minimum(c + 2, last), e, masked)
            return carry

        lax.fori_loop(low // 2, high // 2, body, 0)

    def across_x(e, j):
        return remote(
            to_x.at[e - 1, j],
            from_x.at[e - 1, j],
            x_sems.at[0, e - 1, j],
            x_sems.at[1, e - 1, j],
            {"tract": z * nx + lax.rem(x + e, nx)},
        )

    def along_z(e, j):
        return remote(
            to_z.at[e - 1, j],
            from_z.at[e - 1, j],
            z_sems.at[0, e - 1, j],
            z_sems.at[1, e - 1, j],
            {"tract": lax.rem(z + e, nz) * nx + x},
        )

    def send_over_x(e, part):
        for j in range(part * halves, (part + 1) * halves):
            for k in range(nz):
                to_x[e - 1, j, k] = encode(table[e, j, k * reps : (k + 1) * reps, :])
            across_x(e, j).start()

    def send_along_z(part):
        for j in range(part * halves, (part + 1) * halves):
            for e in range(1, nx):
                across_x(e, j).wait_recv()
            for k in range(nz):
                value = table[0, j, k * reps : (k + 1) * reps, :]
                for e in range(1, nx):
                    value = value + decode(from_x[e - 1, j, k])
                over_x[j, k] = value
            for e in range(1, nz):
                to_z[e - 1, j] = encode(over_x[j, lax.rem(z + e, nz)])
                along_z(e, j).start()

    table[...] = jnp.zeros_like(table)
    for e in range(1, nx):
        for part in range(2):
            mask(0, e, masked)
            if e > 1 or part > 0:
                table_loop(e, part * halves, halves, 0, blocks * quarters)
            else:
                for b in range(blocks):
                    if b + 1 < blocks and (b + 1) % 2 == 1:
                        for q in range(quarters):
                            arrived = other_copies[q][0] if b == 0 else other_relay[q][b // 2 - 1]
                            arrived.wait_recv()
                    following = b + 1 if b + 1 < blocks else None
                    table_loop(e, 0, halves, b * quarters, (b + 1) * quarters, following)
            send_over_x(e, part)
    for part in range(2):
        mask(0, 0, masked)
        table_loop(0, part * halves, halves, 0, blocks * quarters)
        send_along_z(part)
    for j in range(pieces_j):
        value = over_x[j, z]
        for e in range(1, nz):
            along_z(e, j).wait_recv()
            value = value + decode(from_z[e - 1, j])
        tab_ref[0, :, j * lanes : (j + 1) * lanes] = value / scale
    tab_copy = pltpu.make_async_copy(tab_ref, tab_hbm, tab_sem)
    tab_copy.start()

    cal_copy.wait()
    tab_copy.wait()
    for copy in about_copies + about_relay + sum(other_copies + other_relay, []):
        copy.wait_send()
    for c in range(2):
        to_sister(c).wait_send()

    def left(peer):
        @pl.when(peer < tiles)
        def _():
            remote(
                gram.at[core, peer], from_chip.at[chip], send_chip.at[peer], recv_chip.at[chip],
                chip_at(peer),
            ).wait_send()

        @pl.when(chip < tiles)
        def _():
            remote(
                final.at[core, chip], final.at[core, chip], send_back.at[peer], recv_back.at[chip],
                chip_at(peer),
            ).wait_send()

    each_other(chips, left)
    for t in range(tiles):
        hand_over(t).wait_send()
    for j in range(pieces_j):
        for e in range(1, nx):
            across_x(e, j).wait_send()
        for e in range(1, nz):
            along_z(e, j).wait_send()


def finish_kernel(cal_ref, tab_ref, cal_out, tab_out, cal, tab, sems):
    reps = cal_ref.shape[0]
    copy = pltpu.make_async_copy
    arriving, leaving = [], []
    for first in range(0, reps, 8):
        rows, at = slice(first, first + 8), first // 8
        arriving.append(copy(cal_ref.at[rows], cal.at[rows], sems.at[0, at]))
        leaving.append(copy(cal.at[rows], cal_out.at[rows], sems.at[1, at]))
    arriving.append(copy(tab_ref, tab, sems.at[0, reps // 8]))
    leaving.append(copy(tab, tab_out, sems.at[1, reps // 8]))
    for come in arriving:
        come.start()
    for come, go in zip(arriving, leaving):
        come.wait()
        go.start()
    for go in leaving:
        go.wait()


def finish(calibrated, tables):
    return pl.pallas_call(
        finish_kernel,
        in_specs=[pl.BlockSpec(memory_space=pltpu.HBM)] * 2,
        out_specs=[pl.BlockSpec(memory_space=pltpu.HBM)] * 2,
        out_shape=[
            jax.ShapeDtypeStruct(calibrated.shape, f32),
            jax.ShapeDtypeStruct(tables.shape, f32),
        ],
        scratch_shapes=[
            pltpu.VMEM(calibrated.shape, f32),
            pltpu.VMEM(tables.shape, f32),
            pltpu.SemaphoreType.DMA((2, calibrated.shape[0] // 8 + 1)),
        ],
        compiler_params=pltpu.CompilerParams(vmem_limit_bytes=vmem_bytes),
    )(calibrated, tables)


def shards(rep_weights, covariate_codes, tract_of, log_income, controls, threshold_grid):
    reps, people = rep_weights.shape
    variables = covariate_codes.shape[0]
    tracts = lax.axis_size("tract")
    recs = lax.axis_size("rec")
    ny = recs // 2
    nz = 4
    nx = tracts // nz
    chips = ny * tracts
    share = threshold_grid.shape[0] // recs
    pieces_j = share // lanes
    quarters = people // quarter
    size = controls.shape[0]
    rows = pair_layout(variables)[2]
    tiles = -(-rows // lanes)
    cut = pair_layout(variables)[0][1, 2] // lanes
    most = max(cut, tiles - cut) * lanes
    designs = variables * base_levels
    vmem = pltpu.VMEM
    dma = pltpu.SemaphoreType.DMA
    calibrated, tables = pl.pallas_call(
        functools.partial(kernel, ny, tracts, nx, float(people * recs)),
        in_specs=[pl.BlockSpec(memory_space=pltpu.HBM)] + [pl.BlockSpec(memory_space=vmem)] * 5,
        out_specs=[pl.BlockSpec(memory_space=pltpu.HBM)] * 2,
        out_shape=[
            jax.ShapeDtypeStruct((reps, people), f32),
            jax.ShapeDtypeStruct((1, reps, share), f32),
        ],
        scratch_shapes=[
            vmem((reps, people), f32),
            vmem((1, reps, share), f32),
            dma((quarters,)),
            dma,
            dma,
            vmem((3 * reps, people), bf16),
            vmem((most, gram_block), bf16),
            vmem((3 * reps, most), f32),
            vmem((2, tiles, reps // 2, lanes), f32),
            vmem((tiles, reps // 2, lanes), f32),
            vmem((chips, reps // 2, lanes), f32),
            vmem((2, tiles, reps // 2, lanes), f32),
            vmem((tiles * lanes, reps), f32),
            vmem((size, size, reps), f32),
            vmem((size, reps), f32),
            vmem((8, size, reps), f32),
            vmem((size, reps), f32),
            vmem((3 * designs, reps), bf16),
            vmem((recs, 16, people // 2), bf16),
            vmem((people // quarter, reps, quarter), jnp.int16),
            vmem((recs - 1, people // quarter, reps, quarter), jnp.int16),
            vmem((recs * quarters, 8, quarter), f32),
            vmem((8, lanes), f32),
            vmem((share, lanes), f32),
            vmem((recs * quarters, share, quarter), bf16),
            vmem((recs * quarters, designs, quarter), bf16),
            vmem((recs * quarters, reps, quarter), bf16),
            vmem((nz * reps, quarter), bf16),
            vmem((nz * reps, quarter), bf16),
            vmem((nx, pieces_j, nz * reps, lanes), f32),
            vmem((nx - 1, pieces_j, nz, reps + 16, lanes), jnp.int16),
            vmem((nx - 1, pieces_j, nz, reps + 16, lanes), jnp.int16),
            vmem((pieces_j, nz, reps, lanes), f32),
            vmem((nz - 1, pieces_j, reps + 16, lanes), jnp.int16),
            vmem((nz - 1, pieces_j, reps + 16, lanes), jnp.int16),
            dma((2, recs)),
            dma((people // quarter, 2, recs)),
            dma((2, 2)),
            dma((tiles,)),
            dma((chips,)),
            dma((chips,)),
            dma((tiles,)),
            dma((2, tiles)),
            dma((2, nx - 1, pieces_j)),
            dma((2, nz - 1, pieces_j)),
        ],
        compiler_params=pltpu.CompilerParams(
            vmem_limit_bytes=vmem_bytes, collective_id=0, has_side_effects=True
        ),
    )(
        rep_weights,
        covariate_codes,
        tract_of.reshape(1, people),
        log_income.reshape(-1, lanes),
        controls.reshape(1, size),
        threshold_grid.reshape(-1, lanes),
    )
    return finish(calibrated, tables)


def solution(mesh):
    placed = (
        P(None, ("rec", "tract")),
        P(None, ("rec", "tract")),
        P(("rec", "tract"), None),
        P(("rec", "tract")),
        P(),
        P(),
    )
    return jax.shard_map(
        shards,
        mesh=mesh,
        in_specs=placed,
        out_specs=(P(None, ("rec", "tract")), P("tract", None, "rec")),
        check_vma=False,
    )
```

```python
import functools

import jax
import jax.numpy as jnp
from jax import lax
from jax.experimental import pallas as pl
from jax.experimental.pallas import tpu as pltpu
from jax.sharding import PartitionSpec as P

smooth_width = 3.0 / 8192.0
grid_middle = 2048.0
grid_step = 3.0 / 2048.0
half_scale = 0.5 / smooth_width
base_levels = 16
first_kept = 4
kept = base_levels - first_kept
lanes = 128
bf16 = jnp.bfloat16
f32 = jnp.float32
vmem_bytes = 60 * 1024 * 1024


def firsts_of(variables):
    return [0] + [first_kept] * (variables - 1)


def pair_layout(variables):
    offsets, row = {}, 0
    for u, first in enumerate(firsts_of(variables)):
        for v in range(u + 1, variables):
            offsets[u, v] = row
            row += (base_levels - first) * kept
    return offsets, row, row + base_levels


def split3(value, axis):
    high = value.astype(bf16)
    rest = value - high.astype(f32)
    middle = rest.astype(bf16)
    low = (rest - middle.astype(f32)).astype(bf16)
    return jnp.concatenate([high, middle, low], axis=axis)


def one_hot(key, rows):
    row = lax.broadcasted_iota(jnp.int32, (rows, key.shape[1]), 0)
    return jnp.where(row == key, 1.0, 0.0).astype(bf16)


def remote(source, target, send_sem, recv_sem, where):
    return pltpu.make_async_remote_copy(
        src_ref=source,
        dst_ref=target,
        send_sem=send_sem,
        recv_sem=recv_sem,
        device_id=where,
        device_id_type=pl.DeviceIdType.MESH,
    )


def encode(value):
    top = jnp.max(jnp.max(jnp.abs(value), axis=0, keepdims=True), axis=1, keepdims=True)
    power = jnp.ceil(jnp.log2(jnp.maximum(top, 1e-30)))
    coded = jnp.round(value * (code_top * jnp.exp2(-power)))
    power = jnp.broadcast_to(power, (16, value.shape[1]))
    return jnp.concatenate([coded, power], axis=0).astype(jnp.int32).astype(jnp.int16)


def decode(coded):
    coded = coded.astype(jnp.int32).astype(f32)
    reps = coded.shape[0] - 16
    return coded[:reps] * (jnp.exp2(coded[reps : reps + 1]) * (1.0 / code_top))


def solve(variables, sums, aims, mat, rhs, coef, sol):
    size = mat.shape[0]
    offsets, singles, _ = pair_layout(variables)
    firsts = firsts_of(variables)
    starts = [0] + [base_levels + kept * (v - 1) for v in range(1, variables)]
    mat[...] = jnp.zeros_like(mat)
    for v in range(variables):
        count = base_levels - firsts[v]
        if v == 0:
            single = sums[singles : singles + count, :]
        else:
            at = offsets[0, v]
            single = sums[at : at + kept, :]
            for c in range(1, base_levels):
                single = single + sums[at + c * kept : at + (c + 1) * kept, :]
        rhs[starts[v] : starts[v] + count, :] = (
            aims[starts[v] : starts[v] + count, :] - single
        )
        for c in range(count):
            mat[starts[v] + c, starts[v] + c : starts[v] + c + 1, :] = single[c : c + 1, :]
    for (u, v), row in offsets.items():
        for c in range(base_levels - firsts[u]):
            at = row + c * kept
            mat[starts[u] + c, starts[v] : starts[v] + kept, :] = sums[at : at + kept, :]

    inverses = []
    for low in range(0, size, 8):
        rows = [mat[low + p, low:, :] for p in range(8)]
        right = rhs[low:, :]
        place = lax.broadcasted_iota(jnp.int32, rows[0].shape, 0)
        for p in range(8):
            inverse = 1.0 / rows[p][p : p + 1, :]
            factor = jnp.where(place > p, rows[p] * inverse, 0.0)
            coef[p, low:, :] = factor
            for q in range(p + 1, 8):
                rows[q] = rows[q] - factor[q : q + 1, :] * rows[p]
            right = right - factor * right[p : p + 1, :]
            inverses.append(inverse)
        rhs[low:, :] = right
        for p in range(8):
            mat[low + p, low:, :] = rows[p]
        for other in range(low + 8, size, 8):

            def update(pair, carry, low=low, other=other):
                for i in (other + 2 * pair, other + 2 * pair + 1):
                    value = mat[i, other:, :]
                    for p in range(8):
                        value = value - coef[p, pl.ds(i, 1), :] * mat[low + p, other:, :]
                    mat[i, other:, :] = value
                return carry

            lax.fori_loop(0, 4, update, 0)

    for low in reversed(range(0, size, 8)):
        known = []
        for p in range(8):
            value = rhs[low + p : low + p + 1, :]
            if low + 8 < size:
                later = mat[low + p, low + 8 :, :] * sol[low + 8 :, :]
                value = value - jnp.sum(later, axis=0, keepdims=True)
            known.append(value)
        for p in reversed(range(8)):
            found = known[p] * inverses[low + p]
            sol[low + p : low + p + 1, :] = found
            for q in range(p):
                known[q] = known[q] - mat[low + q, low + p : low + p + 1, :] * found

    parts = []
    for v in range(variables):
        count = base_levels - firsts[v]
        if firsts[v]:
            parts.append(jnp.zeros((firsts[v], sol.shape[1]), f32))
        parts.append(sol[starts[v] : starts[v] + count, :])
    return jnp.concatenate(parts, axis=0)


gram_block = 1024
quarter = 1024
low_weight, high_weight = 0.5, 2.0
code_step = (high_weight - low_weight) / 65535.0
code_top = 32000.0


def kernel(
    ny, tracts, nx, scale,
    w_hbm, codes_ref, tract_ref, income_ref, controls_ref, grid_ref,
    cal_hbm, tab_hbm,
    w_ref, tab_ref, w_sems, cal_sem, tab_sem,
    pieces, pairs, acc, gram, from_sister, from_chip, final, sums, mat, rhs, coef, sol, x3,
    about, coded, others, located, corner, cen, smooth, design, sent, masked, masked_too, table,
    to_x, from_x, over_x, to_z, from_z,
    about_sems, other_sems, sister_sems, send_chip, recv_chip, send_back, recv_back,
    final_sems, x_sems, z_sems,
):
    reps, people = w_ref.shape
    variables = codes_ref.shape[0]
    quarters = people // quarter
    nz = tracts // nx
    blocks = 2 * ny
    chips = ny * tracts
    half = reps // 2
    tiles = gram.shape[1]
    offsets, singles, rows = pair_layout(variables)
    firsts = firsts_of(variables)
    share = smooth.shape[1]
    pieces_j = share // lanes

    loads = [
        pltpu.make_async_copy(
            w_hbm.at[:, q * quarter : (q + 1) * quarter],
            w_ref.at[:, q * quarter : (q + 1) * quarter],
            w_sems.at[q],
        )
        for q in range(quarters)
    ]
    for load in loads:
        load.start()

    rec, tract = lax.axis_index("rec"), lax.axis_index("tract")
    y, core = lax.div(rec, 2), lax.rem(rec, 2)
    z, x = lax.div(tract, nx), lax.rem(tract, nx)
    sister = {"rec": 2 * y + 1 - core}
    shift = tracts - 2
    chip = y * tracts + lax.rem(tract + shift, tracts)

    def chip_at(number):
        return {
            "rec": 2 * lax.div(number, tracts) + core,
            "tract": lax.rem(lax.rem(number, tracts) + tracts - shift, tracts),
        }

    def each_other(count, body):
        def step(d, carry):
            body(lax.rem(chip + d, count))
            return carry

        lax.fori_loop(1, count, step, 0)

    barrier = pltpu.get_barrier_semaphore()
    pl.semaphore_signal(barrier, inc=1, device_id=sister, device_id_type=pl.DeviceIdType.MESH)
    each_other(
        chips,
        lambda peer: pl.semaphore_signal(
            barrier, inc=1, device_id=chip_at(peer), device_id_type=pl.DeviceIdType.MESH
        ),
    )

    income = income_ref[...].astype(f32)
    for q in range(quarters):
        cols = slice(q * quarter, (q + 1) * quarter)
        located[q, 0:variables, :] = codes_ref[:, cols].astype(f32)
        located[q, variables : variables + 1, :] = tract_ref[:, cols].astype(f32)
        for i in range(quarter // lanes):
            row = q * (quarter // lanes) + i
            located[q, variables + 1 : variables + 2, i * lanes : (i + 1) * lanes] = income[
                row : row + 1, :
            ]
        located[q, variables + 2 :, :] = jnp.zeros(
            (located.shape[1] - variables - 2, quarter), f32
        )
    for q in range(quarters // 2):
        about[0, :, q * quarter : (q + 1) * quarter] = jnp.concatenate(
            [located[q], located[quarters // 2 + q]], axis=0
        ).astype(bf16)
    for q in range(quarters):
        loads[q].wait()
        part = w_ref[:, q * quarter : (q + 1) * quarter]
        coded[q] = jnp.round((part - low_weight) / code_step - 32768.0).astype(jnp.int32).astype(jnp.int16)
    pieces[...] = split3(w_ref[...], 0)

    def spread(source, slot, sems):
        return [remote(source, slot(1), sems.at[0, 1], sems.at[1, 1], sister)] + [
            remote(
                source,
                slot(2 * e),
                sems.at[0, 2 * e],
                sems.at[1, 2 * e],
                {"rec": 2 * lax.rem(y - e + ny, ny) + core},
            )
            for e in range(1, ny)
        ]

    def relay(slot, sems):
        return [
            remote(
                slot(2 * e), slot(2 * e + 1), sems.at[0, 2 * e + 1], sems.at[1, 2 * e + 1], sister
            )
            for e in range(1, ny)
        ]

    about_slot = lambda b: about.at[b]
    def other_slot(q):
        return lambda b: others.at[b - 1, q]

    about_copies = spread(about.at[0], about_slot, about_sems)
    other_copies = [
        spread(coded.at[q], other_slot(q), other_sems.at[q]) for q in range(quarters)
    ]
    about_relay = relay(about_slot, about_sems)
    other_relay = [relay(other_slot(q), other_sems.at[q]) for q in range(quarters)]
    def start_over_y(first, last):
        for q in range(first, last):
            for copy in other_copies[q][1:]:
                copy.start()


    cut = offsets[1, 2] // lanes
    chunks = [(0, cut), (cut, tiles)]

    def gram_chunk(first, last):
        low, high = first * lanes, last * lanes
        groups = []
        for (u, v), row in offsets.items():
            if low <= row < high:
                groups.append((u, v, row - low, (base_levels - firsts[u]) * kept))
        acc[:, : high - low] = jnp.zeros((acc.shape[0], high - low), f32)

        def body(i, carry):
            cols = pl.ds(pl.multiple_of(i * gram_block, gram_block), gram_block)
            for u, v, row, count in groups:
                right = codes_ref[v : v + 1, cols] - first_kept
                key = (codes_ref[u : u + 1, cols] - firsts[u]) * kept + right
                key = jnp.where(right < 0, -1, key)
                pairs[row : row + count, :] = one_hot(key, count)
            if low <= singles < high:
                pairs[singles - low : high - low, :] = one_hot(
                    codes_ref[0:1, cols], high - singles
                )
            acc[:, : high - low] += lax.dot_general(
                pieces[:, cols],
                pairs[: high - low, :],
                (((1,), (1,)), ((), ())),
                preferred_element_type=f32,
            )
            return carry

        lax.fori_loop(0, people // gram_block, body, 0)
        for t in range(first, last):
            at = slice((t - first) * lanes, (t - first + 1) * lanes)
            value = acc[:reps, at] + acc[reps : 2 * reps, at] + acc[2 * reps :, at]
            gram[0, t] = value[:half]
            gram[1, t] = value[half:]

    def to_sister(c):
        first, last = chunks[c]
        return remote(
            gram.at[1 - core, first:last],
            from_sister.at[first:last],
            sister_sems.at[0, c],
            sister_sems.at[1, c],
            sister,
        )

    def to_chips(c):
        first, last = chunks[c]
        to_sister(c).wait_recv()
        for t in range(first, last):
            gram[core, t] = gram[core, t] + from_sister[t]

        def start(peer):
            @pl.when((peer >= first) & (peer < last))
            def _():
                remote(
                    gram.at[core, peer],
                    from_chip.at[chip],
                    send_chip.at[peer],
                    recv_chip.at[chip],
                    chip_at(peer),
                ).start()

        each_other(chips, start)

    def smooth_part(b):
        if b > 0:
            for q in range(quarters // 2):
                value = about[b, :, q * quarter : (q + 1) * quarter].astype(f32)
                located[b * quarters + q] = value[:8]
                located[b * quarters + quarters // 2 + q] = value[8:]

        def body(q, carry):
            c = b * quarters + q
            income = located[c, variables + 1 : variables + 2, :] * half_scale
            for i in range(quarter // lanes):
                at = slice(i * lanes, (i + 1) * lanes)
                smooth[c, :, at] = (0.5 + 0.5 * jnp.tanh(cen[...] - income[:, at])).astype(bf16)
            for v in range(variables):
                code = located[c, v : v + 1, :].astype(jnp.int32)
                design[c, v * base_levels : (v + 1) * base_levels, :] = one_hot(code, base_levels)
            return carry

        lax.fori_loop(0, quarters, body, 0)

    gram_chunk(*chunks[0])
    gram_chunk(*chunks[1])
    pl.semaphore_wait(barrier, chips)
    to_sister(0).start()
    to_sister(1).start()
    for copy in about_copies[1:] + about_copies[:1]:
        copy.start()
    start_over_y(0, 1)
    to_chips(0)

    corner[...] = jnp.zeros_like(corner)
    count = share // lanes
    corner[:count, :] = (
        (grid_ref[pl.ds(rec * count, count), :].astype(f32) - grid_middle)
        * (grid_step * half_scale)
    )
    corner[count : count + 1, : controls_ref.shape[1]] = controls_ref[...]
    turned = corner[...].T
    for i in range(count):
        cen[i * lanes : (i + 1) * lanes, :] = jnp.broadcast_to(turned[:, i : i + 1], (lanes, lanes))

    size = mat.shape[0]
    aims = jnp.broadcast_to(turned[:size, count : count + 1], (size, reps))
    to_chips(1)
    start_over_y(1, quarters // 2)
    smooth_part(0)
    for e in range(1, ny):
        about_copies[e].wait_recv()
        about_relay[e - 1].start()

    @pl.when(chip < tiles)
    def _():
        each_other(
            chips,
            lambda peer: remote(
                gram.at[core, 0], from_chip.at[peer], send_chip.at[0], recv_chip.at[peer], sister
            ).wait_recv(),
        )
        total = lax.fori_loop(
            1,
            chips,
            lambda d, value: value + from_chip[lax.rem(chip + d, chips)],
            gram[core, chip],
        )
        final[core, chip] = total
        each_other(
            chips,
            lambda peer: remote(
                final.at[core, chip],
                final.at[core, chip],
                send_back.at[peer],
                recv_back.at[chip],
                chip_at(peer),
            ).start(),
        )

    about_copies[0].wait_recv()
    smooth_part(1)

    def hand_over(t):
        return remote(
            final.at[core, t], final.at[core, t], final_sems.at[0, t], final_sems.at[1, t], sister
        )

    def taken(t):
        return remote(
            final.at[core, t],
            final.at[1 - core, t],
            final_sems.at[0, t],
            final_sems.at[1, t],
            sister,
        )

    for t in range(tiles):
        @pl.when(chip != t)
        def _():
            remote(
                final.at[core, t], final.at[core, t], send_back.at[0], recv_back.at[t], sister
            ).wait_recv()

        hand_over(t).start()
    start_over_y(quarters // 2, quarters)
    for q in range(quarters):
        other_copies[q][0].start()
    for e in range(1, ny):
        smooth_part(2 * e)
        about_relay[e - 1].wait_recv()
        smooth_part(2 * e + 1)
    for t in range(tiles):
        taken(t).wait_recv()
        whole = jnp.concatenate([final[0, t], final[1, t]], axis=0)
        sums[t * lanes : (t + 1) * lanes, :] = whole.T

    def relay_over_y(first, last):
        for q in range(first, last):
            for e in range(1, ny):
                other_copies[q][e].wait_recv()
                other_relay[q][e - 1].start()

    relay_over_y(0, quarters // 2)
    x3[...] = split3(solve(variables, sums, aims, mat, rhs, coef, sol), 0)
    relay_over_y(quarters // 2, quarters)

    def factors(c):
        return 1.0 + lax.dot_general(
            x3[...],
            jnp.concatenate([design[c]] * 3, axis=0),
            (((0,), (0,)), ((), ())),
            preferred_element_type=f32,
        )

    def own_weights(q, carry):
        cols = pl.ds(pl.multiple_of(q * quarter, quarter), quarter)
        calibrated = w_ref[:, cols] * factors(q)
        w_ref[:, cols] = calibrated
        sent[q] = calibrated.astype(bf16)
        return carry

    lax.fori_loop(0, quarters, own_weights, 0, unroll=True)
    cal_copy = pltpu.make_async_copy(w_ref, cal_hbm, cal_sem)
    cal_copy.start()

    def other_weights(b, q):
        code = others[b - 1, q].astype(jnp.int32).astype(f32)
        weights = (code + 32768.0) * code_step + low_weight
        sent[b * quarters + q] = (weights * factors(b * quarters + q)).astype(bf16)

    halves = pieces_j // 2

    def mask(c, e, target):
        own = located[c, variables : variables + 1, :]
        value = sent[c]
        for k in range(nz):
            place = (k * nx + lax.rem(x + e, nx)).astype(f32)
            inside = jnp.where(own == place, 1.0, 0.0).astype(bf16)
            target[k * reps : (k + 1) * reps, :] = value * inside

    def add_product(c, source, e, first, count):
        product = lax.dot_general(
            source[...],
            smooth[c, first * lanes : (first + count) * lanes, :],
            (((1,), (1,)), ((), ())),
            preferred_element_type=f32,
        )
        for j in range(count):
            table[e, first + j] += product[:, j * lanes : (j + 1) * lanes]

    last = blocks * quarters - 1

    def table_loop(e, first, count, low, high, b=None):
        def body(i, carry):
            c = 2 * i
            add_product(c, masked, e, first, count)
            mask(c + 1, e, masked_too)
            if b is not None:
                other_weights(b, c - (b - 1) * quarters)
            add_product(c + 1, masked_too, e, first, count)
            if b is not None:
                other_weights(b, c + 1 - (b - 1) * quarters)
            mask(jnp.minimum(c + 2, last), e, masked)
            return carry

        lax.fori_loop(low // 2, high // 2, body, 0)

    def across_x(e, j):
        return remote(
            to_x.at[e - 1, j],
            from_x.at[e - 1, j],
            x_sems.at[0, e - 1, j],
            x_sems.at[1, e - 1, j],
            {"tract": z * nx + lax.rem(x + e, nx)},
        )

    def along_z(e, j):
        return remote(
            to_z.at[e - 1, j],
            from_z.at[e - 1, j],
            z_sems.at[0, e - 1, j],
            z_sems.at[1, e - 1, j],
            {"tract": lax.rem(z + e, nz) * nx + x},
        )

    def send_over_x(e, part):
        for j in range(part * halves, (part + 1) * halves):
            for k in range(nz):
                to_x[e - 1, j, k] = encode(table[e, j, k * reps : (k + 1) * reps, :])
            across_x(e, j).start()

    def send_along_z(part):
        for j in range(part * halves, (part + 1) * halves):
            for e in range(1, nx):
                across_x(e, j).wait_recv()
            for k in range(nz):
                value = table[0, j, k * reps : (k + 1) * reps, :]
                for e in range(1, nx):
                    value = value + decode(from_x[e - 1, j, k])
                over_x[j, k] = value
            for e in range(1, nz):
                to_z[e - 1, j] = encode(over_x[j, lax.rem(z + e, nz)])
                along_z(e, j).start()

    table[...] = jnp.zeros_like(table)
    for e in range(1, nx):
        for part in range(2):
            mask(0, e, masked)
            if e > 1 or part > 0:
                table_loop(e, part * halves, halves, 0, blocks * quarters)
            else:
                for b in range(blocks):
                    if b + 1 < blocks and (b + 1) % 2 == 1:
                        for q in range(quarters):
                            arrived = other_copies[q][0] if b == 0 else other_relay[q][b // 2 - 1]
                            arrived.wait_recv()
                    following = b + 1 if b + 1 < blocks else None
                    table_loop(e, 0, halves, b * quarters, (b + 1) * quarters, following)
            send_over_x(e, part)
    for part in range(2):
        mask(0, 0, masked)
        table_loop(0, part * halves, halves, 0, blocks * quarters)
        send_along_z(part)
    for j in range(pieces_j):
        value = over_x[j, z]
        for e in range(1, nz):
            along_z(e, j).wait_recv()
            value = value + decode(from_z[e - 1, j])
        tab_ref[0, :, j * lanes : (j + 1) * lanes] = value / scale
    tab_copy = pltpu.make_async_copy(tab_ref, tab_hbm, tab_sem)
    tab_copy.start()

    cal_copy.wait()
    tab_copy.wait()
    for copy in about_copies + about_relay + sum(other_copies + other_relay, []):
        copy.wait_send()
    for c in range(2):
        to_sister(c).wait_send()

    def left(peer):
        @pl.when(peer < tiles)
        def _():
            remote(
                gram.at[core, peer], from_chip.at[chip], send_chip.at[peer], recv_chip.at[chip],
                chip_at(peer),
            ).wait_send()

        @pl.when(chip < tiles)
        def _():
            remote(
                final.at[core, chip], final.at[core, chip], send_back.at[peer], recv_back.at[chip],
                chip_at(peer),
            ).wait_send()

    each_other(chips, left)
    for t in range(tiles):
        hand_over(t).wait_send()
    for j in range(pieces_j):
        for e in range(1, nx):
            across_x(e, j).wait_send()
        for e in range(1, nz):
            along_z(e, j).wait_send()


def finish_kernel(cal_ref, tab_ref, cal_out, tab_out, cal, tab, sems):
    reps = cal_ref.shape[0]
    copy = pltpu.make_async_copy
    arriving, leaving = [], []
    for first in range(0, reps, 8):
        rows, at = slice(first, first + 8), first // 8
        arriving.append(copy(cal_ref.at[rows], cal.at[rows], sems.at[0, at]))
        leaving.append(copy(cal.at[rows], cal_out.at[rows], sems.at[1, at]))
    arriving.append(copy(tab_ref, tab, sems.at[0, reps // 8]))
    leaving.append(copy(tab, tab_out, sems.at[1, reps // 8]))
    for come in arriving:
        come.start()
    for come, go in zip(arriving, leaving):
        come.wait()
        go.start()
    for go in leaving:
        go.wait()


def finish(calibrated, tables):
    return pl.pallas_call(
        finish_kernel,
        in_specs=[pl.BlockSpec(memory_space=pltpu.HBM)] * 2,
        out_specs=[pl.BlockSpec(memory_space=pltpu.HBM)] * 2,
        out_shape=[
            jax.ShapeDtypeStruct(calibrated.shape, f32),
            jax.ShapeDtypeStruct(tables.shape, f32),
        ],
        scratch_shapes=[
            pltpu.VMEM(calibrated.shape, f32),
            pltpu.VMEM(tables.shape, f32),
            pltpu.SemaphoreType.DMA((2, calibrated.shape[0] // 8 + 1)),
        ],
        compiler_params=pltpu.CompilerParams(vmem_limit_bytes=vmem_bytes),
    )(calibrated, tables)


def shards(rep_weights, covariate_codes, tract_of, log_income, controls, threshold_grid):
    reps, people = rep_weights.shape
    variables = covariate_codes.shape[0]
    tracts = lax.axis_size("tract")
    recs = lax.axis_size("rec")
    ny = recs // 2
    nz = 4
    nx = tracts // nz
    chips = ny * tracts
    share = threshold_grid.shape[0] // recs
    pieces_j = share // lanes
    quarters = people // quarter
    size = controls.shape[0]
    rows = pair_layout(variables)[2]
    tiles = -(-rows // lanes)
    cut = pair_layout(variables)[0][1, 2] // lanes
    most = max(cut, tiles - cut) * lanes
    designs = variables * base_levels
    vmem = pltpu.VMEM
    dma = pltpu.SemaphoreType.DMA
    calibrated, tables = pl.pallas_call(
        functools.partial(kernel, ny, tracts, nx, float(people * recs)),
        in_specs=[pl.BlockSpec(memory_space=pltpu.HBM)] + [pl.BlockSpec(memory_space=vmem)] * 5,
        out_specs=[pl.BlockSpec(memory_space=pltpu.HBM)] * 2,
        out_shape=[
            jax.ShapeDtypeStruct((reps, people), f32),
            jax.ShapeDtypeStruct((1, reps, share), f32),
        ],
        scratch_shapes=[
            vmem((reps, people), f32),
            vmem((1, reps, share), f32),
            dma((quarters,)),
            dma,
            dma,
            vmem((3 * reps, people), bf16),
            vmem((most, gram_block), bf16),
            vmem((3 * reps, most), f32),
            vmem((2, tiles, reps // 2, lanes), f32),
            vmem((tiles, reps // 2, lanes), f32),
            vmem((chips, reps // 2, lanes), f32),
            vmem((2, tiles, reps // 2, lanes), f32),
            vmem((tiles * lanes, reps), f32),
            vmem((size, size, reps), f32),
            vmem((size, reps), f32),
            vmem((8, size, reps), f32),
            vmem((size, reps), f32),
            vmem((3 * designs, reps), bf16),
            vmem((recs, 16, people // 2), bf16),
            vmem((people // quarter, reps, quarter), jnp.int16),
            vmem((recs - 1, people // quarter, reps, quarter), jnp.int16),
            vmem((recs * quarters, 8, quarter), f32),
            vmem((8, lanes), f32),
            vmem((share, lanes), f32),
            vmem((recs * quarters, share, quarter), bf16),
            vmem((recs * quarters, designs, quarter), bf16),
            vmem((recs * quarters, reps, quarter), bf16),
            vmem((nz * reps, quarter), bf16),
            vmem((nz * reps, quarter), bf16),
            vmem((nx, pieces_j, nz * reps, lanes), f32),
            vmem((nx - 1, pieces_j, nz, reps + 16, lanes), jnp.int16),
            vmem((nx - 1, pieces_j, nz, reps + 16, lanes), jnp.int16),
            vmem((pieces_j, nz, reps, lanes), f32),
            vmem((nz - 1, pieces_j, reps + 16, lanes), jnp.int16),
            vmem((nz - 1, pieces_j, reps + 16, lanes), jnp.int16),
            dma((2, recs)),
            dma((people // quarter, 2, recs)),
            dma((2, 2)),
            dma((tiles,)),
            dma((chips,)),
            dma((chips,)),
            dma((tiles,)),
            dma((2, tiles)),
            dma((2, nx - 1, pieces_j)),
            dma((2, nz - 1, pieces_j)),
        ],
        compiler_params=pltpu.CompilerParams(
            vmem_limit_bytes=vmem_bytes, collective_id=0, has_side_effects=True
        ),
    )(
        rep_weights,
        covariate_codes,
        tract_of.reshape(1, people),
        log_income.reshape(-1, lanes),
        controls.reshape(1, size),
        threshold_grid.reshape(-1, lanes),
    )
    return finish(calibrated, tables)


def solution(mesh):
    placed = (
        P(None, ("rec", "tract")),
        P(None, ("rec", "tract")),
        P(("rec", "tract"), None),
        P(("rec", "tract")),
        P(),
        P(),
    )
    return jax.shard_map(
        shards,
        mesh=mesh,
        in_specs=placed,
        out_specs=(P(None, ("rec", "tract")), P("tract", None, "rec")),
        check_vma=False,
    )
```
